32 devices in a mesh: dp: 4 (over y, x), vocab: 4 (over z), mp: 2 (over core).
Axes of the slice: x: 2, y: 2, z: 4, core: 2. Of those that a mesh axis runs over, the one named last changes fastest.
Arguments:
- hidden: bfloat16 [512, 3584], P('dp', 'mp'), may hold values from -20 to 20
- head_weight: bfloat16 [3584, 152064], P('mp', ('dp', 'vocab')), may hold values from -1 to 1
- teacher_logits: bfloat16 [512, 152064], P('mp', ('dp', 'vocab')), may hold values from -20 to 330
- response_start: int32 [2], replicated, may hold values from 0 to 128
Outputs:
- token_kl: float32 [512], P('mp')
- grad_hidden: float32 [512, 3584], P('dp', 'mp')
- grad_head: bfloat16 [3584, 152064], P('mp', ('dp', 'vocab'))
The draws below stay inside these ranges and needn't reach their ends.
All inputs are finite; a program needn't handle non-finite values.
Results may differ from the reference program's by a relative error of at most 0.01.
Values may be sent and summed in bfloat16 or wider, within the bound.
No kernel may reach another device: no remote copies, remote signals or barrier semaphores. Data moves between devices by JAX's collectives and lax.ppermute only.
A program may use at most 128 MiB of HBM per device.

```python
import jax
import jax.numpy as jnp

D = 3584
V = 152064
LEN = 256
TOKENS = 512
SEQS = 2


def draw_hidden(key, part):
    noise_draw = jnp.clip(jax.random.normal(jax.random.fold_in(key, 11), (TOKENS, D), jnp.float32), -6.0, 6.0)
    return noise_draw.astype(jnp.bfloat16)


def draw_head_weight(key, part):
    weights = 0.05 * jnp.clip(jax.random.normal(jax.random.fold_in(key, 17), (D, V), jnp.float32), -6.0, 6.0)
    return weights.astype(jnp.bfloat16)


def draw_teacher_logits(key, part):
    base_draw = 3.0 * jnp.clip(jax.random.normal(jax.random.fold_in(key, 19), (TOKENS, V), jnp.float32), -6.0, 6.0)
    return base_draw.astype(jnp.bfloat16)


def setup_inputs(seed: int = 0) -> dict:
    keys = jax.random.split(jax.random.key(seed), 5)
    return {
        "hidden": draw_hidden(jax.random.fold_in(keys[4], 71), 0),
        "head_weight": draw_head_weight(jax.random.fold_in(keys[4], 71), 0),
        "teacher_logits": draw_teacher_logits(jax.random.fold_in(keys[4], 71), 0),
        "response_start": jax.random.randint(keys[3], (SEQS,), 0, LEN // 2 + 1).astype(jnp.int32),
    }


def reference(hidden, head_weight, teacher_logits, response_start):
    student = jnp.dot(hidden, head_weight, preferred_element_type=jnp.float32)
    target = teacher_logits.astype(jnp.float32)
    top_s = jnp.max(student, axis=1, keepdims=True)
    top_t = jnp.max(target, axis=1, keepdims=True)
    exp_s = jnp.exp(student - top_s)
    exp_t = jnp.exp(target - top_t)
    sum_s = jnp.sum(exp_s, axis=1)
    sum_t = jnp.sum(exp_t, axis=1)
    cross_term = jnp.sum(exp_t * (target - student), axis=1)
    positions = jnp.arange(TOKENS, dtype=jnp.int32)
    sequence = positions // LEN
    starts = response_start[sequence]
    response_mask = (positions % LEN >= starts).astype(jnp.float32)
    token_kl = response_mask * (cross_term / sum_t - top_t[:, 0] - jnp.log(sum_t) + top_s[:, 0] + jnp.log(sum_s))
    logit_grads = (response_mask[:, None] * (exp_s / sum_s[:, None] - exp_t / sum_t[:, None])).astype(jnp.bfloat16)
    grad_head = jnp.dot(hidden.T, logit_grads, preferred_element_type=jnp.float32).astype(jnp.bfloat16)
    grad_hidden = jnp.dot(logit_grads, head_weight.T, preferred_element_type=jnp.float32)
    return token_kl, grad_hidden, grad_head
```

```python
import functools

import jax
import jax.numpy as jnp
from jax import lax
from jax.experimental import pallas as pl
from jax.experimental.pallas import tpu as pltpu
from jax.sharding import PartitionSpec as P

LEN = 256
F32 = jnp.float32
BF16 = jnp.bfloat16
MIB = 1 << 20


def divide(total, parts):
    return parts if total % (16 * parts) == 0 else 1


def tile_of(rows, want):
    for size in range(min(want, rows) // 16 * 16, 0, -16):
        if rows % size == 0:
            return size
    return rows


def params(mib):
    return pltpu.CompilerParams(
        dimension_semantics=("arbitrary",), vmem_limit_bytes=mib * MIB
    )


def cost(flops, moved, exps=0):
    return pl.CostEstimate(flops=int(flops), bytes_accessed=int(moved), transcendentals=int(exps))


def whole(shape):
    return pl.BlockSpec(shape, lambda i: (0,) * len(shape))


def student_body(hidden_ref, head_ref, *out_refs):
    width = out_refs[0].shape[1]
    full = lax.dot_general(
        head_ref[...], hidden_ref[...], (((1,), (1,)), ((), ())), preferred_element_type=F32
    )
    for k, out_ref in enumerate(out_refs):
        out_ref[...] = full[:, k * width : (k + 1) * width]


def student_chunk(ordered, head_t, first, rows, owners):
    tokens, depth = ordered.shape
    width = tokens // owners
    tile = tile_of(rows, 528)
    base = first // tile
    return pl.pallas_call(
        student_body,
        grid=(rows // tile,),
        in_specs=[
            whole((tokens, depth)),
            pl.BlockSpec((tile, depth), lambda i: (i + base, 0)),
        ],
        out_specs=[pl.BlockSpec((tile, width), lambda i: (i, 0))] * owners,
        out_shape=[jax.ShapeDtypeStruct((rows, width), F32)] * owners,
        compiler_params=params(32),
        cost_estimate=cost(
            2 * rows * tokens * depth, 2 * rows * depth + 2 * tokens * depth + 4 * rows * tokens
        ),
        name="student_chunk",
    )(ordered, head_t)


def totals_body(count, *refs):
    parts = refs[:count]
    teacher_ref, before_ref, out_ref = refs[count:]

    @pl.when(pl.program_id(0) == 0)
    def _():
        out_ref[...] = before_ref[...]

    student = parts[0][...]
    for part in parts[1:]:
        student = student + part[...]
    target = teacher_ref[...].astype(F32)
    old_s, old_t = out_ref[0:1], out_ref[1:2]
    top_s = jnp.maximum(old_s, jnp.max(student, axis=0, keepdims=True))
    top_t = jnp.maximum(old_t, jnp.max(target, axis=0, keepdims=True))
    exp_t = jnp.exp(target - top_t)
    scale_s = jnp.exp(old_s - top_s)
    scale_t = jnp.exp(old_t - top_t)
    sum_s = jnp.sum(jnp.exp(student - top_s), axis=0, keepdims=True)
    sum_t = jnp.sum(exp_t, axis=0, keepdims=True)
    cross = jnp.sum(exp_t * (target - student), axis=0, keepdims=True)
    out_ref[2:3] = out_ref[2:3] * scale_s + sum_s
    out_ref[3:4] = out_ref[3:4] * scale_t + sum_t
    out_ref[4:5] = out_ref[4:5] * scale_t + cross
    out_ref[0:1] = top_s
    out_ref[1:2] = top_t


def totals_chunk(parts, teacher_t, first, before):
    rows, width = parts[0].shape
    tile = tile_of(rows, 528)
    base = first // tile
    return pl.pallas_call(
        functools.partial(totals_body, len(parts)),
        grid=(rows // tile,),
        in_specs=[pl.BlockSpec((tile, width), lambda i: (i, 0))] * len(parts)
        + [pl.BlockSpec((tile, width), lambda i: (i + base, 0)), whole((8, width))],
        out_specs=whole((8, width)),
        out_shape=jax.ShapeDtypeStruct((8, width), F32),
        compiler_params=params(16),
        cost_estimate=cost(
            12 * rows * width, (4 * len(parts) + 2) * rows * width, 2 * rows * width
        ),
        name="totals_chunk",
    )(*parts, teacher_t, before)


def merge(refs):
    rows = [ref[...] for ref in refs]
    top_s = functools.reduce(jnp.maximum, [x[0:1] for x in rows])
    top_t = functools.reduce(jnp.maximum, [x[1:2] for x in rows])
    terms = []
    for x in rows:
        scale_s = jnp.exp(x[0:1] - top_s)
        scale_t = jnp.exp(x[1:2] - top_t)
        terms.append([x[2:3] * scale_s, x[3:4] * scale_t, x[4:5] * scale_t])
    while len(terms) > 1:
        terms = [
            [a + b for a, b in zip(left, right)] for left, right in zip(terms[::2], terms[1::2])
        ]
    return [top_s, top_t] + terms[0]


def merge_body(*refs):
    *in_refs, out_ref = refs
    for row, value in enumerate(merge(in_refs)):
        out_ref[row : row + 1] = value


def finish_body(*refs):
    *in_refs, mask_ref, coef_ref, kl_ref = refs
    top_s, top_t, sum_s, sum_t, cross = merge(in_refs)
    mask = mask_ref[...]
    coef_ref[...] = jnp.zeros(coef_ref.shape, F32)
    coef_ref[0:1] = top_s
    coef_ref[1:2] = top_t
    coef_ref[2:3] = mask / sum_s
    coef_ref[3:4] = mask / sum_t
    kl_ref[...] = mask * (cross / sum_t - top_t - jnp.log(sum_t) + top_s + jnp.log(sum_s))


def merge_call(values, mask=None):
    shape = values[0].shape
    out = jax.ShapeDtypeStruct(shape, F32)
    if mask is None:
        return pl.pallas_call(merge_body, out_shape=out, name="merge_totals")(*values)
    kl = jax.ShapeDtypeStruct((1, shape[1]), F32)
    return pl.pallas_call(finish_body, out_shape=(out, kl), name="finish_totals")(*values, mask)


def own_body(count, last, has_acc, *refs):
    parts = refs[:count]
    teacher_ref, coef_ref, head_ref = refs[count : count + 3]
    rest = refs[count + 3 :]
    before_ref = rest[0] if has_acc else None
    grads_ref, out_ref, acc_ref = rest[1:] if has_acc else rest

    student = parts[0][...]
    for part in parts[1:]:
        student = student + part[...]
    target = teacher_ref[...].astype(F32)
    grads = (
        jnp.exp(student - coef_ref[0:1]) * coef_ref[2:3]
        - jnp.exp(target - coef_ref[1:2]) * coef_ref[3:4]
    ).astype(BF16)
    grads_ref[...] = grads
    add_product(grads, head_ref, before_ref, out_ref, acc_ref)


def add_product(grads, head_ref, before_ref, out_ref, acc_ref):
    step = pl.program_id(0)
    term = lax.dot_general(
        grads, head_ref[...], (((0,), (0,)), ((), ())), preferred_element_type=F32
    )

    @pl.when(step == 0)
    def _():
        acc_ref[...] = term if before_ref is None else before_ref[...] + term

    @pl.when(step > 0)
    def _():
        acc_ref[...] += term

    @pl.when(step == pl.num_programs(0) - 1)
    def _():
        out_ref[...] = acc_ref[...].astype(out_ref.dtype)


def own_chunk(parts, teacher_t, coef, head_t, first, before, last):
    rows, width = parts[0].shape
    depth = head_t.shape[1]
    tile = tile_of(rows, 1056)
    base = first // tile
    has_acc = before is not None
    block = pl.BlockSpec((tile, width), lambda i: (i, 0))
    specs = [block] * len(parts) + [
        pl.BlockSpec((tile, width), lambda i: (i + base, 0)),
        whole((8, width)),
        pl.BlockSpec((tile, depth), lambda i: (i + base, 0)),
    ]
    return pl.pallas_call(
        functools.partial(own_body, len(parts), last, has_acc),
        grid=(rows // tile,),
        in_specs=specs + [whole((width, depth))] * has_acc,
        out_specs=[block, whole((width, depth))],
        out_shape=[
            jax.ShapeDtypeStruct((rows, width), BF16),
            jax.ShapeDtypeStruct((width, depth), BF16 if last else F32),
        ],
        scratch_shapes=[pltpu.VMEM((width, depth), F32)],
        compiler_params=params(40),
        cost_estimate=cost(
            2 * rows * width * depth,
            (4 * len(parts) + 4) * rows * width + 2 * rows * depth,
            2 * rows * width,
        ),
        name="own_grads_chunk",
    )(*parts, teacher_t, coef, head_t, *([before] if has_acc else []))


def other_body(has_acc, grads_ref, head_ref, *rest):
    before_ref = rest[0] if has_acc else None
    out_ref, acc_ref = rest[1:] if has_acc else rest
    add_product(grads_ref[...], head_ref, before_ref, out_ref, acc_ref)


def other_chunk(grads, head_t, first, before, last):
    rows, width = grads.shape
    depth = head_t.shape[1]
    tile = tile_of(rows, 1056)
    base = first // tile
    has_acc = before is not None
    return pl.pallas_call(
        functools.partial(other_body, has_acc),
        grid=(rows // tile,),
        in_specs=[
            pl.BlockSpec((tile, width), lambda i: (i, 0)),
            pl.BlockSpec((tile, depth), lambda i: (i + base, 0)),
        ]
        + [whole((width, depth))] * has_acc,
        out_specs=whole((width, depth)),
        out_shape=jax.ShapeDtypeStruct((width, depth), BF16 if last else F32),
        scratch_shapes=[pltpu.VMEM((width, depth), F32)],
        compiler_params=params(40),
        cost_estimate=cost(2 * rows * width * depth, 2 * rows * (depth + width)),
        name="other_grads_chunk",
    )(grads, head_t, *([before] if has_acc else []))


def head_body(count, hidden_ref, *refs):
    grads = jnp.concatenate([ref[...] for ref in refs[:count]], axis=1)
    out_ref = refs[-1]
    out_ref[...] = jnp.dot(grads, hidden_ref[...], preferred_element_type=F32).astype(BF16)


def head_chunk(ordered, grads, first, total, before):
    rows, width = grads[0].shape
    tokens, depth = ordered.shape
    tile = tile_of(rows, 528)
    base = first // tile
    count = len(grads)
    specs = [whole((tokens, depth))] + [pl.BlockSpec((tile, width), lambda i: (i, 0))] * count
    extra, aliases = [], {}
    if before is not None:
        specs.append(pl.BlockSpec(memory_space=pl.ANY))
        extra, aliases = [before], {count + 1: 0}
    return pl.pallas_call(
        functools.partial(head_body, count),
        grid=(rows // tile,),
        in_specs=specs,
        out_specs=pl.BlockSpec((tile, depth), lambda i: (i + base, 0)),
        out_shape=jax.ShapeDtypeStruct((total, depth), BF16),
        input_output_aliases=aliases,
        compiler_params=params(32),
        cost_estimate=cost(
            2 * rows * tokens * depth, 2 * rows * depth + 2 * tokens * depth + 2 * rows * tokens
        ),
        name="grad_head_chunk",
    )(ordered, *grads, *extra)


def swap(x, axis, k):
    n = lax.axis_size(axis)
    return lax.ppermute(x, axis, [(i, i ^ k) for i in range(n)])


def merge_over(totals, axis, mask=None):
    n = lax.axis_size(axis)
    step = 1
    while step < n:
        span = min(4, n // step)
        values = [totals] + [swap(totals, axis, k * step) for k in range(1, span)]
        step *= span
        totals = merge_call(values, mask if step == n else None)
    return totals


def reduce_rows(partial, k, shard):
    n_dp, n_mp, n_v = lax.axis_size("dp"), lax.axis_size("mp"), lax.axis_size("vocab")
    span = n_dp // n_mp
    inner = lax.axis_index("dp") % span
    flat = lambda j, i, m: (j * span + i) * n_mp + m
    total = partial.astype(F32)
    for a in range(1, n_mp):
        pairs = [
            (flat(m ^ k ^ a, i, m), flat(m ^ k, i, m)) for i in range(span) for m in range(n_mp)
        ]
        total = total + lax.ppermute(partial, ("dp", "mp"), pairs).astype(F32)
    kept = lax.dynamic_slice_in_dim(total, inner * shard, shard)
    for b in range(1, span):
        pairs = [
            (flat(m ^ k, i, m), flat(m ^ k, i ^ b, m)) for i in range(span) for m in range(n_mp)
        ]
        sent = lax.dynamic_slice_in_dim(total, (inner ^ b) * shard, shard).astype(BF16)
        kept = kept + lax.ppermute(sent, ("dp", "mp"), pairs).astype(F32)
    if n_v > 4 or shard % n_v:
        return lax.psum(kept, "vocab")
    part = shard // n_v
    mine = lax.axis_index("vocab")
    axes = ("dp", "vocab", "mp")
    place = lambda j, i, v, m: ((j * span + i) * n_v + v) * n_mp + m
    pairs = [
        [
            (place(m ^ k, i, v, m), place(m ^ k, i, v ^ c, m))
            for i in range(span)
            for v in range(n_v)
            for m in range(n_mp)
        ]
        for c in range(n_v)
    ]
    cut = lambda c: lax.dynamic_slice_in_dim(kept, (mine ^ c) * part, part)
    block = cut(0)
    for c in range(1, n_v):
        block = block + lax.ppermute(cut(c).astype(BF16), axes, pairs[c]).astype(F32)
    block = block.astype(BF16)
    result = jnp.zeros((shard, partial.shape[1]), F32)
    for c in range(n_v):
        piece = lax.ppermute(block, axes, pairs[c]) if c else block
        result = lax.dynamic_update_slice_in_dim(result, piece.astype(F32), (mine ^ c) * part, 0)
    return result


def per_device(hidden, head_weight, teacher_logits, response_start):
    n_dp, n_mp = lax.axis_size("dp"), lax.axis_size("mp")
    span = n_dp // n_mp
    shard, depth = hidden.shape
    own_rows, columns = teacher_logits.shape
    mp = lax.axis_index("mp")
    dp = lax.axis_index("dp")
    head_t = head_weight.T
    teacher_t = teacher_logits.T

    positions = mp * own_rows + jnp.arange(own_rows, dtype=jnp.int32)
    sequence = positions // LEN
    seq_ids = jnp.arange(response_start.shape[0], dtype=jnp.int32)
    starts = jnp.sum(
        jnp.where(sequence[:, None] == seq_ids[None, :], response_start[None, :], 0), axis=1
    )
    mask = (positions % LEN >= starts).astype(F32)[None, :]

    ordered = jnp.zeros((n_dp * shard, depth), BF16)
    for k in range(n_dp):
        block = swap(hidden, "dp", k) if k else hidden
        source = dp ^ k
        place = ((source // span) ^ mp) * span + source % span
        ordered = lax.dynamic_update_slice_in_dim(ordered, block, place * shard, 0)

    chunks = divide(columns, 3)
    rows = columns // chunks
    firsts = [c * rows for c in range(chunks)]

    parts = []
    for first in firsts:
        outs = student_chunk(ordered, head_t, first, rows, n_mp)
        parts.append([outs[0]] + [swap(outs[k], "mp", k) for k in range(1, n_mp)])

    totals = jnp.concatenate(
        [jnp.full((2, own_rows), -jnp.inf, F32), jnp.zeros((6, own_rows), F32)]
    )
    for first, part in zip(firsts, parts):
        totals = totals_chunk(part, teacher_t, first, totals)
    totals = merge_over(totals, "dp")
    coef, token_kl = merge_over(totals, "vocab", mask)

    grads = []
    acc = None
    for c, first in enumerate(firsts):
        own, acc = own_chunk(parts[c], teacher_t, coef, head_t, first, acc, c == chunks - 1)
        grads.append([own] + [swap(own, "mp", k) for k in range(1, n_mp)])
    grad_hidden = reduce_rows(acc, 0, shard)
    for k in range(1, n_mp):
        acc = None
        for c, first in enumerate(firsts):
            acc = other_chunk(grads[c][k], head_t, first, acc, c == chunks - 1)
        reduced = reduce_rows(acc, k, shard)
        grad_hidden = jnp.where(dp // span == (mp ^ k), reduced, grad_hidden)

    grad_head = None
    for c, first in enumerate(firsts):
        grad_head = head_chunk(ordered, grads[c], first, columns, grad_head)
    return (token_kl.reshape(own_rows), grad_hidden, grad_head.T)


def solution(mesh):
    return jax.shard_map(
        per_device,
        mesh=mesh,
        in_specs=(P("dp", "mp"), P("mp", ("dp", "vocab")), P("mp", ("dp", "vocab")), P()),
        out_specs=(P("mp"), P("dp", "mp"), P("mp", ("dp", "vocab"))),
        check_vma=False,
    )
```

```python
import functools

import jax
import jax.numpy as jnp
from jax import lax
from jax.experimental import pallas as pl
from jax.experimental.pallas import tpu as pltpu
from jax.sharding import PartitionSpec as P

LEN = 256
F32 = jnp.float32
BF16 = jnp.bfloat16
MIB = 1 << 20
LARGE = 63
WEIGHT = 1 / 16


def divide(total, parts, unit):
    return parts if total % (unit * parts) == 0 else 1


def tile_of(rows, want):
    for size in range(min(want, rows) // 16 * 16, 0, -16):
        if rows % size == 0:
            return size
    return rows


def params(mib):
    return pltpu.CompilerParams(
        dimension_semantics=("arbitrary",), vmem_limit_bytes=mib * MIB
    )


def cost(flops, moved, exps=0):
    return pl.CostEstimate(
        flops=int(flops * WEIGHT),
        bytes_accessed=int(moved * WEIGHT),
        transcendentals=int(exps * WEIGHT),
    )


def whole(shape):
    return pl.BlockSpec(shape, lambda i: (0,) * len(shape))


def fold(op, x, sub):
    if sub == 1:
        return op(x, axis=0, keepdims=True)
    return op(x.reshape(x.shape[0] // sub, sub, x.shape[1]), axis=0)


def spread(op, x, row, sub):
    if sub == 1:
        return op(x, row)
    rows, width = x.shape
    return op(x.reshape(rows // sub, sub, width), row[None]).reshape(rows, width)


def add_totals(parts, teacher_ref, state_ref, sub):
    student = parts[0][...]
    for part in parts[1:]:
        student = student + part[...]
    target = teacher_ref[...].astype(F32)
    old = [state_ref[sub * r : sub * (r + 1)] for r in range(5)]
    top_s = jnp.maximum(old[0], fold(jnp.max, student, sub))
    top_t = jnp.maximum(old[1], fold(jnp.max, target, sub))
    exp_s = jnp.exp(spread(jnp.subtract, student, top_s, sub))
    exp_t = jnp.exp(spread(jnp.subtract, target, top_t, sub))
    scale_s = jnp.exp(old[0] - top_s)
    scale_t = jnp.exp(old[1] - top_t)
    new = [
        top_s,
        top_t,
        old[2] * scale_s + fold(jnp.sum, exp_s, sub),
        old[3] * scale_t + fold(jnp.sum, exp_t, sub),
        old[4] * scale_t + fold(jnp.sum, exp_t * (target - student), sub),
    ]
    for r, value in enumerate(new):
        state_ref[sub * r : sub * (r + 1)] = value


def merge_classes(state_ref, sub):
    rows = [state_ref[sub * r : sub * (r + 1)] for r in range(5)]
    top_s = jnp.max(rows[0], axis=0, keepdims=True)
    top_t = jnp.max(rows[1], axis=0, keepdims=True)
    scale_s = jnp.exp(rows[0] - top_s)
    scale_t = jnp.exp(rows[1] - top_t)
    return [
        top_s,
        top_t,
        jnp.sum(rows[2] * scale_s, axis=0, keepdims=True),
        jnp.sum(rows[3] * scale_t, axis=0, keepdims=True),
        jnp.sum(rows[4] * scale_t, axis=0, keepdims=True),
    ]


def start_totals(sub, width):
    return jnp.concatenate(
        [jnp.full((2 * sub, width), -jnp.inf, F32), jnp.zeros((3 * sub, width), F32)]
    )


def totals_step(refs, state_ref, out_ref, sub, last, ready_refs=()):
    *parts, teacher_ref, before_ref = refs
    step = pl.program_id(0)

    @pl.when(step == 0)
    def _():
        state_ref[...] = before_ref[...]

    add_totals(parts, teacher_ref, state_ref, sub)

    @pl.when(step == pl.num_programs(0) - 1)
    def _():
        if last:
            out_ref[...] = jnp.zeros(out_ref.shape, F32)
            for r, value in enumerate(merge_classes(state_ref, sub)):
                out_ref[r : r + 1, out_ref.shape[1] - value.shape[1] :] = value
            at = 0
            for ref in ready_refs:
                out_ref[:, at : at + ref.shape[1]] = ref[...]
                at += ref.shape[1]
        else:
            out_ref[...] = state_ref[...]


def totals_specs(parts, teacher, tile, base, sub, last):
    width = teacher.shape[1]
    place = lambda i: (i + base, 0)
    specs = [pl.BlockSpec((tile, width), lambda i: (i, 0))] * len(parts)
    specs += [pl.BlockSpec((tile, width), place), whole((5 * sub, width))]
    out = (8 if last else 5 * sub, width)
    return specs, whole(out), jax.ShapeDtypeStruct(out, F32), pltpu.VMEM((5 * sub, width), F32)


def student_body(owners, sub, last, has_totals, *refs):
    hidden_ref, head_ref = refs[:2]
    if has_totals:
        totals_refs = refs[2 : -owners - 3]
        out_refs = refs[-owners - 3 : -3]
        totals_ref, hidden_t, state_ref = refs[-3:]
    else:
        out_refs, hidden_t = refs[2:-1], refs[-1]

    @pl.when(pl.program_id(0) == 0)
    def _():
        hidden_t[...] = hidden_ref[...].T

    width = out_refs[0].shape[1]
    full = jnp.dot(head_ref[...], hidden_t[...], preferred_element_type=F32)
    for k, out_ref in enumerate(out_refs):
        out_ref[...] = full[:, k * width : (k + 1) * width]
    if has_totals:
        totals_step(totals_refs, state_ref, totals_ref, sub, last)


def student_chunk(hidden, head_t, first, rows, owners, totals=None):
    tokens, depth = hidden.shape
    width = tokens // owners
    tile = tile_of(rows, 1056)
    steps = rows // tile
    base = first // tile
    specs = [whole((tokens, depth)), pl.BlockSpec((tile, depth), lambda i: (i + base, 0))]
    outs = [pl.BlockSpec((tile, width), lambda i: (i, 0))] * owners
    shapes = [jax.ShapeDtypeStruct((rows, width), F32)] * owners
    scratch = [pltpu.VMEM((depth, tokens), BF16)]
    args = [hidden, head_t]
    sub, last = 1, False
    if totals is not None:
        parts, teacher, before, at, count, last = totals
        sub = before.shape[0] // 5
        size = count // steps
        more, out, shape, state = totals_specs(parts, teacher, size, at // size, sub, last)
        specs += more
        outs = outs + [out]
        shapes = shapes + [shape]
        scratch.append(state)
        args += [*parts, teacher, before]
    return pl.pallas_call(
        functools.partial(student_body, owners, sub, last, totals is not None),
        grid=(steps,),
        in_specs=specs,
        out_specs=outs,
        out_shape=shapes,
        scratch_shapes=scratch,
        compiler_params=params(LARGE),
        cost_estimate=cost(
            2 * rows * tokens * depth, 2 * rows * depth + 2 * tokens * depth + 4 * rows * tokens
        ),
        name="student_chunk",
    )(*args)


def totals_body(sub, last, ready, *refs):
    *in_refs, out_ref, state_ref = refs
    split = len(in_refs) - ready
    totals_step(in_refs[:split], state_ref, out_ref, sub, last, in_refs[split:])


def totals_chunk(parts, teacher, first, before, last, ready):
    rows, width = parts[0].shape
    ready = ready if last else []
    sub = before.shape[0] // 5
    tile = tile_of(rows, 1056)
    specs, out, shape, state = totals_specs(parts, teacher, tile, first // tile, sub, last)
    if last:
        out = whole((8, width * (len(ready) + 1)))
        shape = jax.ShapeDtypeStruct(out.block_shape, F32)
    return pl.pallas_call(
        functools.partial(totals_body, sub, last, len(ready)),
        grid=(rows // tile,),
        in_specs=specs + [whole(r.shape) for r in ready],
        out_specs=out,
        out_shape=shape,
        scratch_shapes=[state],
        compiler_params=params(LARGE),
        cost_estimate=cost(
            12 * rows * width, (4 * len(parts) + 2) * rows * width, 2 * rows * width
        ),
        name="totals_chunk",
    )(*parts, teacher, before, *ready)


def merge(refs, shifts, width):
    rows = []
    for ref, shift in zip(refs, shifts):
        x = ref[...]
        if shift:
            cut = [x[:, at : at + width] for at in range(0, x.shape[1], width)]
            x = jnp.concatenate([cut[w ^ shift] for w in range(len(cut))], axis=1)
        rows.append(x)
    top_s = functools.reduce(jnp.maximum, [x[0:1] for x in rows])
    top_t = functools.reduce(jnp.maximum, [x[1:2] for x in rows])
    terms = []
    for x in rows:
        scale_s = jnp.exp(x[0:1] - top_s)
        scale_t = jnp.exp(x[1:2] - top_t)
        terms.append([x[2:3] * scale_s, x[3:4] * scale_t, x[4:5] * scale_t])
    while len(terms) > 1:
        terms = [
            [a + b for a, b in zip(left, right)] for left, right in zip(terms[::2], terms[1::2])
        ]
    return [top_s, top_t] + terms[0]


def merge_body(shifts, width, *refs):
    *in_refs, out_ref = refs
    out_ref[...] = jnp.zeros(out_ref.shape, F32)
    for row, value in enumerate(merge(in_refs, shifts, width)):
        out_ref[row : row + 1] = value


def finish_body(shifts, width, *refs):
    *in_refs, mask_ref, coef_ref, kl_ref = refs
    top_s, top_t, sum_s, sum_t, cross = merge(in_refs, shifts, width)
    mask = mask_ref[...]
    coef_ref[...] = jnp.zeros(coef_ref.shape, F32)
    coef_ref[0:1] = top_s
    coef_ref[1:2] = top_t
    coef_ref[2:3] = mask / sum_s
    coef_ref[3:4] = mask / sum_t
    kl_ref[...] = mask * (cross / sum_t - top_t - jnp.log(sum_t) + top_s + jnp.log(sum_s))


def merge_call(values, shifts, width, mask=None):
    shape = values[0].shape
    out = jax.ShapeDtypeStruct(shape, F32)
    small = pltpu.CompilerParams(vmem_limit_bytes=2 * MIB)
    guess = cost(1 << 20, 1 << 16)
    if mask is None:
        return pl.pallas_call(
            functools.partial(merge_body, shifts, width),
            out_shape=out,
            compiler_params=small,
            cost_estimate=guess,
            name="merge_totals",
        )(*values)
    kl = jax.ShapeDtypeStruct((1, shape[1]), F32)
    return pl.pallas_call(
        functools.partial(finish_body, shifts, width),
        out_shape=(out, kl),
        compiler_params=small,
        cost_estimate=guess,
        name="finish_totals",
    )(*values, mask)


def grads_body(waves, count, *refs):
    coef_ref, out_ref = refs[-2:]
    width = out_ref.shape[1] // waves
    for w in range(waves):
        *parts, teacher_ref = refs[w * (count + 1) : (w + 1) * (count + 1)]
        coef = coef_ref[:, w * width : (w + 1) * width]
        student = parts[0][...]
        for part in parts[1:]:
            student = student + part[...]
        target = teacher_ref[...].astype(F32)
        out_ref[:, w * width : (w + 1) * width] = (
            jnp.exp(student - coef[0:1]) * coef[2:3] - jnp.exp(target - coef[1:2]) * coef[3:4]
        ).astype(BF16)


def grads_chunk(wave_parts, teachers, coef, first, rows):
    total, width = teachers[0].shape
    waves, count = len(wave_parts), len(wave_parts[0])
    tile = tile_of(rows, 1056)
    args = [x for parts, teacher in zip(wave_parts, teachers) for x in (*parts, teacher)]
    return pl.pallas_call(
        functools.partial(grads_body, waves, count),
        grid=(rows // tile,),
        in_specs=chunk_specs(args, tile, first, total) + [whole(coef.shape)],
        out_specs=pl.BlockSpec((tile, waves * width), lambda i: (i, 0)),
        out_shape=jax.ShapeDtypeStruct((rows, waves * width), BF16),
        compiler_params=params(LARGE),
        cost_estimate=cost(
            8 * rows * waves * width,
            (4 * count + 4) * rows * waves * width,
            2 * rows * waves * width,
        ),
        name="logit_grads_chunk",
    )(*args, coef)


def chunk_specs(arrays, tile, first, total):
    return [
        pl.BlockSpec(
            (tile, x.shape[1]),
            functools.partial(lambda base, i: (i + base, 0), first // tile if x.shape[0] == total else 0),
        )
        for x in arrays
    ]


def by_wave(refs, waves):
    width = refs[0].shape[1] // waves
    return [ref[:, w * width : (w + 1) * width] for w in range(waves) for ref in refs]


def hidden_body(count, waves, has_acc, emit, *refs):
    grads_refs, head_ref = refs[:count], refs[count]
    rest = list(refs[count + 1 :])
    before_ref = rest.pop(0) if has_acc else None
    if emit:
        turned_ref, *out_refs, acc_ref = rest
        turned = jnp.concatenate([x.T for x in by_wave(grads_refs, waves)], axis=0)
        turned_ref[0] = turned
    else:
        *out_refs, acc_ref = rest
        turned = grads_refs[0][0]
    step = pl.program_id(0)
    term = jnp.dot(turned, head_ref[...], preferred_element_type=F32)

    @pl.when(step == 0)
    def _():
        acc_ref[...] = term if before_ref is None else before_ref[...] + term

    @pl.when(step > 0)
    def _():
        acc_ref[...] += term

    @pl.when(step == pl.num_programs(0) - 1)
    def _():
        at = 0
        for ref in out_refs:
            ref[...] = acc_ref[at : at + ref.shape[0]].astype(ref.dtype)
            at += ref.shape[0]


def hidden_chunk(grads, head_t, first, rows, waves, part, parts, before, last):
    total, depth = head_t.shape
    size = depth // parts
    emit = part == 0
    tile = rows
    base = first // tile
    if emit:
        tokens = sum(g.shape[1] for g in grads)
        specs = chunk_specs(grads, tile, first, total)
    else:
        tokens = grads[0].shape[1]
        specs = [pl.BlockSpec((1, tokens, tile), lambda i: (i, 0, 0))]
    specs.append(pl.BlockSpec((tile, size), lambda i: (i + base, part)))
    acc = whole((tokens, size))
    pieces = waves if last else 1
    out_specs = [whole((tokens // pieces, size))] * pieces
    out_shape = [jax.ShapeDtypeStruct((tokens // pieces, size), BF16 if last else F32)] * pieces
    if emit:
        out_specs = [pl.BlockSpec((1, tokens, tile), lambda i: (i, 0, 0))] + out_specs
        out_shape = [jax.ShapeDtypeStruct((rows // tile, tokens, tile), BF16)] + out_shape
    has_acc = before is not None
    return pl.pallas_call(
        functools.partial(hidden_body, len(grads), waves, has_acc, emit),
        grid=(rows // tile,),
        in_specs=specs + [acc] * has_acc,
        out_specs=out_specs,
        out_shape=out_shape,
        scratch_shapes=[pltpu.VMEM((tokens, size), F32)],
        compiler_params=params(48),
        cost_estimate=cost(2 * rows * tokens * size, 2 * rows * (size + tokens)),
        name="grad_hidden_chunk",
    )(*grads, head_t, *([before] if has_acc else []))


def head_body(waves, count, *refs):
    hidden_refs, grads_refs = refs[:waves], refs[waves : waves + count]
    out_ref, flag_ref, hidden = refs[-3:]

    @pl.when(pl.program_id(0) == 0)
    def _():
        flag_ref[...] = jnp.zeros(flag_ref.shape, F32)
        at = 0
        for ref in hidden_refs:
            hidden[at : at + ref.shape[0]] = ref[...]
            at += ref.shape[0]

    grads = jnp.concatenate(by_wave(grads_refs, waves), axis=1)
    out_ref[...] = jnp.dot(grads, hidden[...], preferred_element_type=F32).astype(BF16)


def head_chunk(hiddens, grads, first, rows, total, before):
    depth = hiddens[0].shape[1]
    tokens = sum(h.shape[0] for h in hiddens)
    tile = tile_of(rows, 1056)
    base = first // tile
    waves, count = len(hiddens), len(grads)
    specs = [whole(h.shape) for h in hiddens] + chunk_specs(grads, tile, first, total)
    extra, aliases = [], {}
    if before is not None:
        specs.append(pl.BlockSpec(memory_space=pl.ANY))
        extra, aliases = [before], {waves + count: 0}
    return pl.pallas_call(
        functools.partial(head_body, waves, count),
        grid=(rows // tile,),
        in_specs=specs,
        out_specs=[pl.BlockSpec((tile, depth), lambda i: (i + base, 0)), whole((8, 128))],
        out_shape=[
            jax.ShapeDtypeStruct((total, depth), BF16),
            jax.ShapeDtypeStruct((8, 128), F32),
        ],
        scratch_shapes=[pltpu.VMEM((tokens, depth), BF16)],
        input_output_aliases=aliases,
        compiler_params=params(40),
        cost_estimate=cost(
            2 * rows * tokens * depth, 2 * rows * depth + 2 * tokens * depth + 2 * rows * tokens
        ),
        name="grad_head_chunk",
    )(*hiddens, *grads, *extra)


def swap(x, axis, k):
    n = lax.axis_size(axis)
    return lax.ppermute(x, axis, [(i, i ^ k) for i in range(n)])


def merge_over(totals, axis, waves, mask=None):
    n = lax.axis_size(axis)
    width = totals.shape[1] // waves
    step = 1
    while step < n:
        span = min(4, n // step)
        values = [totals] + [swap(totals, axis, k * step) for k in range(1, span)]
        shifts = tuple(k * step % waves if axis == "dp" else 0 for k in range(span))
        step *= span
        totals = merge_call(values, shifts, width, mask if step == n else None)
    return totals


def rows_at(x, index, size):
    return lax.dynamic_slice_in_dim(x, index * size, size)


class Reduction:
    def __init__(self, partial, shard, own):
        self.partial, self.shard, self.own = partial, shard, own
        self.owners = lax.axis_size("mp")
        self.waves = lax.axis_size("dp") // self.owners

    def over_inner(self, flag):
        total = self.partial[0].astype(F32)
        for w in range(1, self.waves):
            total += tie(swap(self.partial[w], "dp", w), flag).astype(F32)
        self.total = total
        return total

    def over_outer(self, flag):
        total = rows_at(self.total, self.own, self.shard)
        for a in range(1, self.owners):
            sent = rows_at(self.total, self.own ^ a, self.shard).astype(BF16)
            total += tie(swap(sent, "dp", a * self.waves), flag).astype(F32)
        self.total = total
        return total

    def scatter_vocab(self, flag):
        n = lax.axis_size("vocab")
        if n > 4 or self.shard % (8 * n):
            self.block = lax.psum(self.total, "vocab")
            return self.block
        mine, size = lax.axis_index("vocab"), self.shard // n
        block = rows_at(self.total, mine, size)
        for c in range(1, n):
            sent = rows_at(self.total, mine ^ c, size).astype(BF16)
            block += tie(swap(sent, "vocab", c), flag).astype(F32)
        self.block = block.astype(BF16)
        return self.block

    def gather_vocab(self, flag):
        if self.block.shape[0] == self.shard:
            return self.block
        n = lax.axis_size("vocab")
        mine, size = lax.axis_index("vocab"), self.shard // n
        result = jnp.zeros(self.total.shape, F32)
        for c in range(n):
            piece = tie(swap(self.block, "vocab", c), flag) if c else self.block
            result = lax.dynamic_update_slice_in_dim(
                result, piece.astype(F32), (mine ^ c) * size, 0
            )
        return result


def tie(x, *after):
    return lax.optimization_barrier((x, *after))[0]


def per_device(hidden, head_weight, teacher_logits, response_start):
    n_dp, n_mp = lax.axis_size("dp"), lax.axis_size("mp")
    waves = n_dp // n_mp
    shard, depth = hidden.shape
    own_rows, columns = teacher_logits.shape
    mp = lax.axis_index("mp")
    dp = lax.axis_index("dp")
    outer, inner = dp // waves, dp % waves
    own = outer ^ mp
    head_t = head_weight.T
    teacher_t = teacher_logits.T

    def in_wave(x, w):
        return lax.dynamic_slice_in_dim(x, (inner ^ w) * shard, shard, axis=1)

    positions = mp * own_rows + jnp.concatenate(
        [(inner ^ w) * shard + jnp.arange(shard, dtype=jnp.int32) for w in range(waves)]
    )
    sequence = positions // LEN
    seq_ids = jnp.arange(response_start.shape[0], dtype=jnp.int32)
    starts = jnp.sum(
        jnp.where(sequence[:, None] == seq_ids[None, :], response_start[None, :], 0), axis=1
    )
    mask = (positions % LEN >= starts).astype(F32)[None, :]
    teachers = [in_wave(teacher_t, w) for w in range(waves)]

    def ordered(blocks):
        result = jnp.zeros((n_mp * shard, depth), BF16)
        for a, block in enumerate(blocks):
            result = lax.dynamic_update_slice_in_dim(result, block, (own ^ a) * shard, 0)
        return result

    first_blocks = [hidden] + [swap(hidden, "dp", a * waves) for a in range(1, n_mp)]
    hiddens = [ordered(first_blocks)]
    for w in range(1, waves):
        hiddens.append(ordered([swap(block, "dp", w) for block in first_blocks]))

    chunks = divide(columns, 3, 16)
    rows = columns // chunks
    firsts = [c * rows for c in range(chunks)]
    sub = 8 if columns % 8 == 0 else 1

    def exchanged(outs):
        return [outs[0]] + [swap(outs[k], "mp", k) for k in range(1, n_mp)]

    wave_parts, ready = [], []
    for w in range(waves):
        parts, before = [], start_totals(sub, shard)
        for c, first in enumerate(firsts):
            states = hiddens[w]
            if w + 1 < waves and c == chunks - 1:
                states = tie(states, hiddens[w + 1])
            beside = None
            if w:
                beside = (wave_parts[-1][c], teachers[w - 1], before, first, rows, c == chunks - 1)
            outs = student_chunk(states, head_t, first, rows, n_mp, beside)
            if w:
                before = outs[n_mp]
            parts.append(exchanged(outs[:n_mp]))
        if w:
            ready.append(before)
        wave_parts.append(parts)
    for w in range(len(ready), waves):
        totals = start_totals(sub, shard)
        for c, part in enumerate(wave_parts[w]):
            last = c == len(wave_parts[w]) - 1
            totals = totals_chunk(
                part, teachers[w], c * rows, totals, last, ready if w == waves - 1 else []
            )
        ready.append(totals)
    totals = merge_over(ready[-1], "dp", waves)
    coef, kl = merge_over(totals, "vocab", waves, mask)
    token_kl = jnp.zeros((1, own_rows), F32)
    for w in range(waves):
        token_kl = lax.dynamic_update_slice_in_dim(
            token_kl, kl[:, w * shard : (w + 1) * shard], (inner ^ w) * shard, 1
        )

    all_grads = []
    for c, first in enumerate(firsts):
        parts = [p[c] for p in wave_parts]
        all_grads.append(exchanged([grads_chunk(parts, teachers, coef, first, rows)] * n_mp))

    halves = divide(depth, 2, 128)
    reductions = []
    turned = [None] * chunks
    for part in range(halves):
        acc = None
        for c, first in enumerate(firsts):
            last = c == chunks - 1
            if part == 0:
                turned[c], *acc = hidden_chunk(
                    all_grads[c], head_t, first, rows, waves, part, halves, acc, last
                )
            else:
                acc = hidden_chunk(
                    [turned[c]], head_t, first, rows, waves, part, halves, acc, last
                )
            if not last:
                (acc,) = acc
        turned[0] = tie(turned[0], *acc)
        reductions.append(Reduction(acc, shard, own))
    results = [reductions[0].over_inner(reductions[-1].partial[0])]
    plan = [
        lambda flag: [reductions[0].over_outer(flag)]
        + [r.over_inner(flag) for r in reductions[1:]],
        lambda flag: [reductions[0].scatter_vocab(flag)]
        + [r.over_outer(flag) for r in reductions[1:]],
        lambda flag: [reductions[0].gather_vocab(flag)]
        + [r.scatter_vocab(flag) for r in reductions[1:]],
    ]
    grad_head = None
    for c, first in enumerate(firsts):
        inputs = [tie(hiddens[0], *results)] + hiddens[1:]
        grad_head, flag = head_chunk(inputs, all_grads[c], first, rows, columns, grad_head)
        if plan:
            results = plan.pop(0)(flag)
    while plan:
        results = plan.pop(0)(flag)
    grad_hidden = jnp.concatenate(
        [results[0]] + [r.gather_vocab(flag) for r in reductions[1:]], axis=1
    )
    return (token_kl.reshape(own_rows), grad_hidden, grad_head.T)


def solution(mesh):
    return jax.shard_map(
        per_device,
        mesh=mesh,
        in_specs=(P("dp", "mp"), P("mp", ("dp", "vocab")), P("mp", ("dp", "vocab")), P()),
        out_specs=(P("mp"), P("dp", "mp"), P("mp", ("dp", "vocab"))),
        check_vma=False,
    )
```

```python
import functools

import jax
import jax.numpy as jnp
from jax import lax
from jax.experimental import pallas as pl
from jax.experimental.pallas import tpu as pltpu
from jax.sharding import PartitionSpec as P

LEN = 256
F32 = jnp.float32
BF16 = jnp.bfloat16
MIB = 1 << 20
LARGE = 63
WEIGHT = 1 / 16
TILE = 528
SLICE = 48
STREAMS = 3


def divide(total, parts, unit):
    return parts if total % (unit * parts) == 0 else 1


def tile_of(rows, want):
    for size in range(min(want, rows) // 16 * 16, 0, -16):
        if rows % size == 0:
            return size
    return rows


def params(mib):
    return pltpu.CompilerParams(
        dimension_semantics=("arbitrary",), vmem_limit_bytes=mib * MIB
    )


def cost(flops, moved, exps=0):
    return pl.CostEstimate(
        flops=int(flops * WEIGHT),
        bytes_accessed=int(moved * WEIGHT),
        transcendentals=int(exps * WEIGHT),
    )


def whole(shape):
    return pl.BlockSpec(shape, lambda i: (0,) * len(shape))


def fold(op, x, sub):
    if sub == 1:
        return op(x, axis=0, keepdims=True)
    return op(x.reshape(x.shape[0] // sub, sub, x.shape[1]), axis=0)


def spread(op, x, row, sub):
    if sub == 1:
        return op(x, row)
    rows, width = x.shape
    return op(x.reshape(rows // sub, sub, width), row[None]).reshape(rows, width)


def slices_of(rows):
    size = tile_of(rows, SLICE)
    return [slice(at, at + size) for at in range(0, rows, size)]


def add_totals(parts, teacher_ref, state_ref, sub):
    state = [state_ref[sub * r : sub * (r + 1)] for r in range(5)]
    for rows in slices_of(teacher_ref.shape[0]):
        student = parts[0][rows]
        for part in parts[1:]:
            student = student + part[rows]
        target = teacher_ref[rows].astype(F32)
        top_s = jnp.maximum(state[0], fold(jnp.max, student, sub))
        top_t = jnp.maximum(state[1], fold(jnp.max, target, sub))
        exp_s = jnp.exp(spread(jnp.subtract, student, top_s, sub))
        exp_t = jnp.exp(spread(jnp.subtract, target, top_t, sub))
        scale_s = jnp.exp(state[0] - top_s)
        scale_t = jnp.exp(state[1] - top_t)
        state = [
            top_s,
            top_t,
            state[2] * scale_s + fold(jnp.sum, exp_s, sub),
            state[3] * scale_t + fold(jnp.sum, exp_t, sub),
            state[4] * scale_t + fold(jnp.sum, exp_t * (target - student), sub),
        ]
    for r, value in enumerate(state):
        state_ref[sub * r : sub * (r + 1)] = value


def merge_classes(state_ref, sub):
    rows = [state_ref[sub * r : sub * (r + 1)] for r in range(5)]
    top_s = jnp.max(rows[0], axis=0, keepdims=True)
    top_t = jnp.max(rows[1], axis=0, keepdims=True)
    scale_s = jnp.exp(rows[0] - top_s)
    scale_t = jnp.exp(rows[1] - top_t)
    return [
        top_s,
        top_t,
        jnp.sum(rows[2] * scale_s, axis=0, keepdims=True),
        jnp.sum(rows[3] * scale_t, axis=0, keepdims=True),
        jnp.sum(rows[4] * scale_t, axis=0, keepdims=True),
    ]


def start_totals(sub, width):
    return jnp.concatenate(
        [jnp.full((2 * sub, width), -jnp.inf, F32), jnp.zeros((3 * sub, width), F32)]
    )


def totals_step(refs, state_ref, out_ref, sub, last, ready_refs=()):
    *parts, teacher_ref, before_ref = refs
    step = pl.program_id(0)

    @pl.when(step == 0)
    def _():
        state_ref[...] = before_ref[...]

    add_totals(parts, teacher_ref, state_ref, sub)

    @pl.when(step == pl.num_programs(0) - 1)
    def _():
        if last:
            out_ref[...] = jnp.zeros(out_ref.shape, F32)
            for r, value in enumerate(merge_classes(state_ref, sub)):
                out_ref[r : r + 1, out_ref.shape[1] - value.shape[1] :] = value
            at = 0
            for ref in ready_refs:
                out_ref[:, at : at + ref.shape[1]] = ref[...]
                at += ref.shape[1]
        else:
            out_ref[...] = state_ref[...]


def totals_specs(parts, teacher, tile, base, sub, last):
    width = teacher.shape[1]
    place = lambda i: (i + base, 0)
    specs = [pl.BlockSpec((tile, width), lambda i: (i, 0))] * len(parts)
    specs += [pl.BlockSpec((tile, width), place), whole((5 * sub, width))]
    out = (8 if last else 5 * sub, width)
    return specs, whole(out), jax.ShapeDtypeStruct(out, F32), pltpu.VMEM((5 * sub, width), F32)


def head_streams(head_t, rows, first, size, part=0):
    count = STREAMS if rows % (16 * STREAMS) == 0 else 1
    step = rows // count
    return [
        pl.BlockSpec(
            (step, size), functools.partial(lambda j, i: (i * count + j, part), first // step + j)
        )
        for j in range(count)
    ]


def student_body(owners, streams, sub, last, has_totals, is_first, *refs):
    refs = list(refs)
    take = lambda count: [refs.pop(0) for _ in range(count)]
    if is_first:
        (own_ref,) = take(1)
        block_refs = take(owners)
    else:
        (turned_ref,) = take(1)
    head_refs = take(streams)
    state_ref = refs.pop() if has_totals else None
    totals_ref = refs.pop() if has_totals else None
    if is_first:
        turned_ref, ordered_ref = refs.pop(), refs.pop()
    out_refs = refs[-owners:]
    totals_refs = refs[:-owners]
    width = out_refs[0].shape[1]

    if is_first:
        for own in range(owners):

            @pl.when((pl.program_id(0) == 0) & (own_ref[0] == own))
            def _():
                for a, ref in enumerate(block_refs):
                    place = slice((own ^ a) * width, ((own ^ a) + 1) * width)
                    ordered_ref[place] = ref[...]
                    turned_ref[:, place] = ref[...].T

    head = jnp.concatenate([ref[...] for ref in head_refs], axis=0)
    full = jnp.dot(head, turned_ref[...], preferred_element_type=F32)
    for k, out_ref in enumerate(out_refs):
        out_ref[...] = full[:, k * width : (k + 1) * width]
    if has_totals:
        totals_step(totals_refs, state_ref, totals_ref, sub, last)


def student_chunk(states, head_t, first, rows, owners, width, totals=None):
    depth = head_t.shape[1]
    tokens = owners * width
    tile = tile_of(rows, TILE)
    steps = rows // tile
    is_first = isinstance(states, tuple)
    if is_first:
        args = [states[0], *states[1]]
        specs = [pl.BlockSpec(memory_space=pltpu.SMEM)] + [whole((width, depth))] * owners
    else:
        args = [states]
        specs = [whole((depth, tokens))]
    streams = head_streams(head_t, tile, first, depth)
    specs += streams
    args += [head_t] * len(streams)
    outs = [pl.BlockSpec((tile, width), lambda i: (i, 0))] * owners
    shapes = [jax.ShapeDtypeStruct((rows, width), F32)] * owners
    if is_first:
        outs = outs + [whole((tokens, depth)), whole((depth, tokens))]
        shapes = shapes + [
            jax.ShapeDtypeStruct((tokens, depth), BF16),
            jax.ShapeDtypeStruct((depth, tokens), BF16),
        ]
    scratch = []
    sub, last = 1, False
    if totals is not None:
        parts, teacher, before, at, count, last = totals
        sub = before.shape[0] // 5
        size = count // steps
        more, out, shape, state = totals_specs(parts, teacher, size, at // size, sub, last)
        specs += more
        outs = outs + [out]
        shapes = shapes + [shape]
        scratch.append(state)
        args += [*parts, teacher, before]
    return pl.pallas_call(
        functools.partial(
            student_body, owners, len(streams), sub, last, totals is not None, is_first
        ),
        grid=(steps,),
        in_specs=specs,
        out_specs=outs,
        out_shape=shapes,
        scratch_shapes=scratch,
        compiler_params=params(LARGE),
        cost_estimate=cost(
            2 * rows * tokens * depth, 2 * rows * depth + 2 * tokens * depth + 4 * rows * tokens
        ),
        name="student_chunk",
    )(*args)


def totals_body(sub, last, ready, *refs):
    *in_refs, out_ref, state_ref = refs
    split = len(in_refs) - ready
    totals_step(in_refs[:split], state_ref, out_ref, sub, last, in_refs[split:])


def totals_chunk(parts, teacher, first, before, last, ready):
    rows, width = parts[0].shape
    ready = ready if last else []
    sub = before.shape[0] // 5
    tile = tile_of(rows, TILE)
    specs, out, shape, state = totals_specs(parts, teacher, tile, first // tile, sub, last)
    if last:
        out = whole((8, width * (len(ready) + 1)))
        shape = jax.ShapeDtypeStruct(out.block_shape, F32)
    return pl.pallas_call(
        functools.partial(totals_body, sub, last, len(ready)),
        grid=(rows // tile,),
        in_specs=specs + [whole(r.shape) for r in ready],
        out_specs=out,
        out_shape=shape,
        scratch_shapes=[state],
        compiler_params=params(LARGE),
        cost_estimate=cost(
            12 * rows * width, (4 * len(parts) + 2) * rows * width, 2 * rows * width
        ),
        name="totals_chunk",
    )(*parts, teacher, before, *ready)


def merge(refs, shifts, width):
    rows = []
    for ref, shift in zip(refs, shifts):
        x = ref[...]
        if shift:
            cut = [x[:, at : at + width] for at in range(0, x.shape[1], width)]
            x = jnp.concatenate([cut[w ^ shift] for w in range(len(cut))], axis=1)
        rows.append(x)
    top_s = functools.reduce(jnp.maximum, [x[0:1] for x in rows])
    top_t = functools.reduce(jnp.maximum, [x[1:2] for x in rows])
    terms = []
    for x in rows:
        scale_s = jnp.exp(x[0:1] - top_s)
        scale_t = jnp.exp(x[1:2] - top_t)
        terms.append([x[2:3] * scale_s, x[3:4] * scale_t, x[4:5] * scale_t])
    while len(terms) > 1:
        terms = [
            [a + b for a, b in zip(left, right)] for left, right in zip(terms[::2], terms[1::2])
        ]
    return [top_s, top_t] + terms[0]


def merge_body(shifts, width, *refs):
    *in_refs, out_ref = refs
    out_ref[...] = jnp.zeros(out_ref.shape, F32)
    for row, value in enumerate(merge(in_refs, shifts, width)):
        out_ref[row : row + 1] = value


def finish_body(shifts, width, *refs):
    *in_refs, mask_ref, coef_ref, kl_ref = refs
    top_s, top_t, sum_s, sum_t, cross = merge(in_refs, shifts, width)
    mask = mask_ref[...]
    coef_ref[...] = jnp.zeros(coef_ref.shape, F32)
    coef_ref[0:1] = top_s
    coef_ref[1:2] = top_t
    coef_ref[2:3] = mask / sum_s
    coef_ref[3:4] = mask / sum_t
    kl_ref[...] = mask * (cross / sum_t - top_t - jnp.log(sum_t) + top_s + jnp.log(sum_s))


def merge_call(values, shifts, width, mask=None):
    shape = values[0].shape
    out = jax.ShapeDtypeStruct(shape, F32)
    small = pltpu.CompilerParams(vmem_limit_bytes=2 * MIB)
    guess = cost(1 << 20, 1 << 16)
    if mask is None:
        return pl.pallas_call(
            functools.partial(merge_body, shifts, width),
            out_shape=out,
            compiler_params=small,
            cost_estimate=guess,
            name="merge_totals",
        )(*values)
    kl = jax.ShapeDtypeStruct((1, shape[1]), F32)
    return pl.pallas_call(
        functools.partial(finish_body, shifts, width),
        out_shape=(out, kl),
        compiler_params=small,
        cost_estimate=guess,
        name="finish_totals",
    )(*values, mask)


def grads_body(waves, count, *refs):
    coef_ref, out_ref = refs[-2:]
    width = out_ref.shape[1] // waves
    for w in range(waves):
        *parts, teacher_ref = refs[w * (count + 1) : (w + 1) * (count + 1)]
        coef = coef_ref[:, w * width : (w + 1) * width]
        for rows in slices_of(out_ref.shape[0]):
            student = parts[0][rows]
            for part in parts[1:]:
                student = student + part[rows]
            target = teacher_ref[rows].astype(F32)
            out_ref[rows, w * width : (w + 1) * width] = (
                jnp.exp(student - coef[0:1]) * coef[2:3]
                - jnp.exp(target - coef[1:2]) * coef[3:4]
            ).astype(BF16)


def grads_chunk(wave_parts, teachers, coef, first, rows):
    total, width = teachers[0].shape
    waves, count = len(wave_parts), len(wave_parts[0])
    tile = tile_of(rows, TILE)
    args = [x for parts, teacher in zip(wave_parts, teachers) for x in (*parts, teacher)]
    return pl.pallas_call(
        functools.partial(grads_body, waves, count),
        grid=(rows // tile,),
        in_specs=chunk_specs(args, tile, first, total) + [whole(coef.shape)],
        out_specs=pl.BlockSpec((tile, waves * width), lambda i: (i, 0)),
        out_shape=jax.ShapeDtypeStruct((rows, waves * width), BF16),
        compiler_params=params(LARGE),
        cost_estimate=cost(
            8 * rows * waves * width,
            (4 * count + 4) * rows * waves * width,
            2 * rows * waves * width,
        ),
        name="logit_grads_chunk",
    )(*args, coef)


def chunk_specs(arrays, tile, first, total):
    return [
        pl.BlockSpec(
            (tile, x.shape[1]),
            functools.partial(lambda base, i: (i + base, 0), first // tile if x.shape[0] == total else 0),
        )
        for x in arrays
    ]


def by_wave(refs, waves):
    width = refs[0].shape[1] // waves
    return [ref[:, w * width : (w + 1) * width] for w in range(waves) for ref in refs]


def hidden_body(count, streams, waves, has_acc, emit, *refs):
    grads_refs, head_refs = refs[:count], refs[count : count + streams]
    rest = list(refs[count + streams :])
    before_ref = rest.pop(0) if has_acc else None
    if emit:
        turned_ref, *out_refs, acc_ref = rest
        turned = jnp.concatenate([x.T for x in by_wave(grads_refs, waves)], axis=0)
        turned_ref[0] = turned
    else:
        *out_refs, acc_ref = rest
        turned = grads_refs[0][0]
    step = pl.program_id(0)
    head = jnp.concatenate([ref[...] for ref in head_refs], axis=0)
    term = jnp.dot(turned, head, preferred_element_type=F32)

    @pl.when(step == 0)
    def _():
        acc_ref[...] = term if before_ref is None else before_ref[...] + term

    @pl.when(step > 0)
    def _():
        acc_ref[...] += term

    @pl.when(step == pl.num_programs(0) - 1)
    def _():
        at = 0
        for ref in out_refs:
            ref[...] = acc_ref[at : at + ref.shape[0]].astype(ref.dtype)
            at += ref.shape[0]


def hidden_chunk(grads, head_t, first, rows, waves, part, parts, before, last):
    total, depth = head_t.shape
    size = depth // parts
    emit = part == 0
    tile = tile_of(rows, 2 * TILE)
    if emit:
        tokens = sum(g.shape[1] for g in grads)
        specs = chunk_specs(grads, tile, first, total)
    else:
        tokens = grads[0].shape[1]
        specs = [pl.BlockSpec((1, tokens, tile), lambda i: (i, 0, 0))]
    streams = head_streams(head_t, tile, first, size, part)
    specs += streams
    acc = whole((tokens, size))
    pieces = waves if last else 1
    out_specs = [whole((tokens // pieces, size))] * pieces
    out_shape = [jax.ShapeDtypeStruct((tokens // pieces, size), BF16 if last else F32)] * pieces
    if emit:
        out_specs = [pl.BlockSpec((1, tokens, tile), lambda i: (i, 0, 0))] + out_specs
        out_shape = [jax.ShapeDtypeStruct((rows // tile, tokens, tile), BF16)] + out_shape
    has_acc = before is not None
    return pl.pallas_call(
        functools.partial(hidden_body, len(grads), len(streams), waves, has_acc, emit),
        grid=(rows // tile,),
        in_specs=specs + [acc] * has_acc,
        out_specs=out_specs,
        out_shape=out_shape,
        scratch_shapes=[pltpu.VMEM((tokens, size), F32)],
        compiler_params=params(48),
        cost_estimate=cost(2 * rows * tokens * size, 2 * rows * (size + tokens)),
        name="grad_hidden_chunk",
    )(*grads, *[head_t] * len(streams), *([before] if has_acc else []))


def head_body(waves, count, *refs):
    hidden_refs, grads_refs = refs[:waves], refs[waves : waves + count]
    out_ref, flag_ref = refs[-2:]

    @pl.when(pl.program_id(0) == 0)
    def _():
        flag_ref[...] = jnp.zeros(flag_ref.shape, F32)

    grads = jnp.concatenate(by_wave(grads_refs, waves), axis=1)
    hidden = jnp.concatenate([ref[...] for ref in hidden_refs], axis=0)
    out_ref[...] = jnp.dot(grads, hidden, preferred_element_type=F32).astype(BF16)


def head_chunk(hiddens, grads, first, rows, total, before):
    depth = hiddens[0].shape[1]
    tokens = sum(h.shape[0] for h in hiddens)
    tile = tile_of(rows, TILE)
    base = first // tile
    waves, count = len(hiddens), len(grads)
    specs = [whole(h.shape) for h in hiddens] + chunk_specs(grads, tile, first, total)
    extra, aliases = [], {}
    if before is not None:
        specs.append(pl.BlockSpec(memory_space=pl.ANY))
        extra, aliases = [before], {waves + count: 0}
    return pl.pallas_call(
        functools.partial(head_body, waves, count),
        grid=(rows // tile,),
        in_specs=specs,
        out_specs=[pl.BlockSpec((tile, depth), lambda i: (i + base, 0)), whole((8, 128))],
        out_shape=[
            jax.ShapeDtypeStruct((total, depth), BF16),
            jax.ShapeDtypeStruct((8, 128), F32),
        ],
        input_output_aliases=aliases,
        compiler_params=params(40),
        cost_estimate=cost(
            2 * rows * tokens * depth, 2 * rows * depth + 2 * tokens * depth + 2 * rows * tokens
        ),
        name="grad_head_chunk",
    )(*hiddens, *grads, *extra)


def swap(x, axis, k):
    n = lax.axis_size(axis)
    return lax.ppermute(x, axis, [(i, i ^ k) for i in range(n)])


def merge_over(totals, axis, waves, mask=None):
    n = lax.axis_size(axis)
    width = totals.shape[1] // waves
    step = 1
    while step < n:
        span = min(4, n // step)
        values = [totals] + [swap(totals, axis, k * step) for k in range(1, span)]
        shifts = tuple(k * step % waves if axis == "dp" else 0 for k in range(span))
        step *= span
        totals = merge_call(values, shifts, width, mask if step == n else None)
    return totals


def rows_at(x, index, size):
    return lax.dynamic_slice_in_dim(x, index * size, size)


class Reduction:
    def __init__(self, partial, shard, own):
        self.partial, self.shard, self.own = partial, shard, own
        self.owners = lax.axis_size("mp")
        self.waves = lax.axis_size("dp") // self.owners

    def over_inner(self, flag):
        total = self.partial[0].astype(F32)
        for w in range(1, self.waves):
            total += tie(swap(self.partial[w], "dp", w), flag).astype(F32)
        self.total = total
        return total

    def over_outer(self, flag):
        total = rows_at(self.total, self.own, self.shard)
        for a in range(1, self.owners):
            sent = rows_at(self.total, self.own ^ a, self.shard).astype(BF16)
            total += tie(swap(sent, "dp", a * self.waves), flag).astype(F32)
        self.total = total
        return total

    def scatter_vocab(self, flag):
        n = lax.axis_size("vocab")
        if n > 4 or self.shard % (8 * n):
            self.block = lax.psum(self.total, "vocab")
            return self.block
        mine, size = lax.axis_index("vocab"), self.shard // n
        block = rows_at(self.total, mine, size)
        for c in range(1, n):
            sent = rows_at(self.total, mine ^ c, size).astype(BF16)
            block += tie(swap(sent, "vocab", c), flag).astype(F32)
        self.block = block.astype(BF16)
        return self.block

    def gather_vocab(self, flag):
        if self.block.shape[0] == self.shard:
            return self.block
        n = lax.axis_size("vocab")
        mine, size = lax.axis_index("vocab"), self.shard // n
        result = jnp.zeros(self.total.shape, F32)
        for c in range(n):
            piece = tie(swap(self.block, "vocab", c), flag) if c else self.block
            result = lax.dynamic_update_slice_in_dim(
                result, piece.astype(F32), (mine ^ c) * size, 0
            )
        return result


def tie(x, *after):
    return lax.optimization_barrier((x, *after))[0]


def per_device(hidden, head_weight, teacher_logits, response_start):
    n_dp, n_mp = lax.axis_size("dp"), lax.axis_size("mp")
    waves = n_dp // n_mp
    shard, depth = hidden.shape
    own_rows, columns = teacher_logits.shape
    mp = lax.axis_index("mp")
    dp = lax.axis_index("dp")
    outer, inner = dp // waves, dp % waves
    own = outer ^ mp
    head_t = head_weight.T
    teacher_t = teacher_logits.T

    def in_wave(x, w):
        return lax.dynamic_slice_in_dim(x, (inner ^ w) * shard, shard, axis=1)

    positions = mp * own_rows + jnp.concatenate(
        [(inner ^ w) * shard + jnp.arange(shard, dtype=jnp.int32) for w in range(waves)]
    )
    sequence = positions // LEN
    seq_ids = jnp.arange(response_start.shape[0], dtype=jnp.int32)
    starts = jnp.sum(
        jnp.where(sequence[:, None] == seq_ids[None, :], response_start[None, :], 0), axis=1
    )
    mask = (positions % LEN >= starts).astype(F32)[None, :]
    teachers = [in_wave(teacher_t, w) for w in range(waves)]

    blocks = [[hidden] + [swap(hidden, "dp", a * waves) for a in range(1, n_mp)]]
    for w in range(1, waves):
        blocks.append([swap(block, "dp", w) for block in blocks[0]])
    blocks[0][0] = tie(hidden, *teachers)

    chunks = divide(columns, 3, 16)
    rows = columns // chunks
    firsts = [c * rows for c in range(chunks)]
    sub = 8 if columns % 8 == 0 else 1

    def exchanged(outs):
        return [outs[0]] + [swap(outs[k], "mp", k) for k in range(1, n_mp)]

    wave_parts, ready, hiddens = [], [], []
    place = own.astype(jnp.int32).reshape(1)
    for w in range(waves):
        parts, before = [], start_totals(sub, shard)
        for c, first in enumerate(firsts):
            states = turned if c else (place, blocks[w])
            if w + 1 < waves and c and c == chunks - 1:
                states = tie(states, *blocks[w + 1])
            beside = None
            if w:
                beside = (wave_parts[-1][c], teachers[w - 1], before, first, rows, c == chunks - 1)
            outs = student_chunk(states, head_t, first, rows, n_mp, shard, beside)
            if w:
                before = outs[-1]
            if c == 0:
                ordered, turned = outs[n_mp : n_mp + 2]
                hiddens.append(ordered)
            parts.append(exchanged(outs[:n_mp]))
        if w:
            ready.append(before)
        wave_parts.append(parts)
    for w in range(len(ready), waves):
        totals = start_totals(sub, shard)
        for c, part in enumerate(wave_parts[w]):
            last = c == len(wave_parts[w]) - 1
            totals = totals_chunk(
                part, teachers[w], c * rows, totals, last, ready if w == waves - 1 else []
            )
        ready.append(totals)
    totals = merge_over(ready[-1], "dp", waves)
    coef, kl = merge_over(totals, "vocab", waves, mask)
    token_kl = jnp.zeros((1, own_rows), F32)
    for w in range(waves):
        token_kl = lax.dynamic_update_slice_in_dim(
            token_kl, kl[:, w * shard : (w + 1) * shard], (inner ^ w) * shard, 1
        )

    all_grads = []
    for c, first in enumerate(firsts):
        parts = [p[c] for p in wave_parts]
        all_grads.append(exchanged([grads_chunk(parts, teachers, coef, first, rows)] * n_mp))

    halves = divide(depth, 2, 128)
    reductions = []
    turned = [None] * chunks
    for part in range(halves):
        acc = None
        for c, first in enumerate(firsts):
            last = c == chunks - 1
            if part == 0:
                turned[c], *acc = hidden_chunk(
                    all_grads[c], head_t, first, rows, waves, part, halves, acc, last
                )
            else:
                acc = hidden_chunk(
                    [turned[c]], head_t, first, rows, waves, part, halves, acc, last
                )
            if not last:
                (acc,) = acc
        turned[0] = tie(turned[0], *acc)
        reductions.append(Reduction(acc, shard, own))
    results = [reductions[0].over_inner(reductions[-1].partial[0])]
    plan = [
        lambda flag: [reductions[0].over_outer(flag)]
        + [r.over_inner(flag) for r in reductions[1:]],
        lambda flag: [reductions[0].scatter_vocab(flag)]
        + [r.over_outer(flag) for r in reductions[1:]],
        lambda flag: [reductions[0].gather_vocab(flag)]
        + [r.scatter_vocab(flag) for r in reductions[1:]],
    ]
    grad_head = None
    for c, first in enumerate(firsts):
        inputs = [tie(hiddens[0], *results)] + hiddens[1:]
        grad_head, flag = head_chunk(inputs, all_grads[c], first, rows, columns, grad_head)
        if plan:
            results = plan.pop(0)(flag)
    while plan:
        results = plan.pop(0)(flag)
    grad_hidden = jnp.concatenate(
        [results[0]] + [r.gather_vocab(flag) for r in reductions[1:]], axis=1
    )
    return (token_kl.reshape(own_rows), grad_hidden, grad_head.T)


def solution(mesh):
    return jax.shard_map(
        per_device,
        mesh=mesh,
        in_specs=(P("dp", "mp"), P("mp", ("dp", "vocab")), P("mp", ("dp", "vocab")), P()),
        out_specs=(P("mp"), P("dp", "mp"), P("mp", ("dp", "vocab"))),
        check_vma=False,
    )
```

```python
import functools

import jax
import jax.numpy as jnp
from jax import lax
from jax.experimental import pallas as pl
from jax.experimental.pallas import tpu as pltpu
from jax.sharding import PartitionSpec as P

LEN = 256
F32 = jnp.float32
BF16 = jnp.bfloat16
MIB = 1 << 20
WEIGHT = 1 / 16
TILE = 528
COLUMNS = 256


def divide(total, parts, unit):
    return parts if total % (unit * parts) == 0 else 1


def tile_of(rows, want):
    for size in range(min(want, rows) // 16 * 16, 0, -16):
        if rows % size == 0:
            return size
    return rows


def params(mib):
    return pltpu.CompilerParams(
        dimension_semantics=("arbitrary",), vmem_limit_bytes=mib * MIB
    )


def cost(flops, moved, exps=0):
    return pl.CostEstimate(
        flops=int(flops * WEIGHT),
        bytes_accessed=int(moved * WEIGHT),
        transcendentals=int(exps * WEIGHT),
    )


def whole(shape):
    return pl.BlockSpec(shape, lambda i: (0,) * len(shape))


def fold(op, x, sub):
    if sub == 1:
        return (jnp.max if op is jnp.maximum else jnp.sum)(x, axis=0, keepdims=True)
    x = x.reshape(x.shape[0] // sub, sub, x.shape[1])
    while x.shape[0] > 1:
        half = x.shape[0] // 2
        rest = x[2 * half :]
        x = op(x[:half], x[half : 2 * half])
        if rest.shape[0]:
            x = jnp.concatenate([x, rest], axis=0)
    return x[0]


def spread(op, x, row, sub):
    if sub == 1:
        return op(x, row)
    rows, width = x.shape
    return op(x.reshape(rows // sub, sub, width), row[None]).reshape(rows, width)


def add_totals(parts, teacher_refs, state_ref, sub):
    student = parts[0][...]
    for part in parts[1:]:
        student = student + part[...]
    target = jnp.concatenate([ref[...] for ref in teacher_refs], axis=1).astype(F32)
    old = [state_ref[sub * r : sub * (r + 1)] for r in range(5)]
    top_s = jnp.maximum(old[0], fold(jnp.maximum, student, sub))
    top_t = jnp.maximum(old[1], fold(jnp.maximum, target, sub))
    exp_s = jnp.exp(spread(jnp.subtract, student, top_s, sub))
    exp_t = jnp.exp(spread(jnp.subtract, target, top_t, sub))
    scale_s = jnp.exp(old[0] - top_s)
    scale_t = jnp.exp(old[1] - top_t)
    new = [
        top_s,
        top_t,
        old[2] * scale_s + fold(jnp.add, exp_s, sub),
        old[3] * scale_t + fold(jnp.add, exp_t, sub),
        old[4] * scale_t + fold(jnp.add, exp_t * (target - student), sub),
    ]
    for r, value in enumerate(new):
        state_ref[sub * r : sub * (r + 1)] = value


def merge_classes(state_ref, sub):
    rows = [state_ref[sub * r : sub * (r + 1)] for r in range(5)]
    top_s = jnp.max(rows[0], axis=0, keepdims=True)
    top_t = jnp.max(rows[1], axis=0, keepdims=True)
    scale_s = jnp.exp(rows[0] - top_s)
    scale_t = jnp.exp(rows[1] - top_t)
    return [
        top_s,
        top_t,
        jnp.sum(rows[2] * scale_s, axis=0, keepdims=True),
        jnp.sum(rows[3] * scale_t, axis=0, keepdims=True),
        jnp.sum(rows[4] * scale_t, axis=0, keepdims=True),
    ]


def start_totals(sub, width):
    return jnp.concatenate(
        [jnp.full((2 * sub, width), -jnp.inf, F32), jnp.zeros((3 * sub, width), F32)]
    )


def totals_body(count, waves, sub, last, *refs):
    parts, teacher_refs = refs[:count], refs[count : count + waves]
    before_ref, out_ref, state_ref = refs[count + waves :]
    step = pl.program_id(0)

    @pl.when(step == 0)
    def _():
        state_ref[...] = before_ref[...]

    add_totals(parts, teacher_refs, state_ref, sub)

    @pl.when(step == pl.num_programs(0) - 1)
    def _():
        if last:
            out_ref[...] = jnp.zeros(out_ref.shape, F32)
            for r, value in enumerate(merge_classes(state_ref, sub)):
                out_ref[r : r + 1] = value
        else:
            out_ref[...] = state_ref[...]


def totals_chunk(parts, teachers, first, before, last):
    rows, width = parts[0].shape
    total = teachers[0].shape[0]
    sub = before.shape[0] // 5
    tile = tile_of(rows, TILE)
    out = (8 if last else 5 * sub, width)
    return pl.pallas_call(
        functools.partial(totals_body, len(parts), len(teachers), sub, last),
        grid=(rows // tile,),
        in_specs=chunk_specs([*parts, *teachers], tile, first, total) + [whole(before.shape)],
        out_specs=whole(out),
        out_shape=jax.ShapeDtypeStruct(out, F32),
        scratch_shapes=[pltpu.VMEM((5 * sub, width), F32)],
        compiler_params=params(12),
        cost_estimate=cost(
            12 * rows * width, (4 * len(parts) + 2) * rows * width, 2 * rows * width
        ),
        name="totals_chunk",
    )(*parts, *teachers, before)


def student_body(owners, places, *refs):
    refs = list(refs)
    if places is not None:
        own_ref = refs.pop(0)
        piece_refs = [refs.pop(0) for _ in places]
        turned_ref, ordered_ref = refs.pop(), refs.pop()

        for own in range(owners):

            @pl.when((pl.program_id(0) == 0) & (own_ref[0] == own))
            def _():
                for (a, at), ref in zip(places, piece_refs):
                    start = (own ^ a) * (ordered_ref.shape[0] // owners) + at
                    ordered_ref[start : start + ref.shape[0]] = ref[...]

        @pl.when(pl.program_id(0) == 0)
        def _():
            turned_ref[...] = ordered_ref[...].T

    else:
        turned_ref = refs.pop(0)
    head_ref, *out_refs = refs
    width = out_refs[0].shape[1]
    full = jnp.dot(head_ref[...], turned_ref[...], preferred_element_type=F32)
    for k, out_ref in enumerate(out_refs):
        out_ref[...] = full[:, k * width : (k + 1) * width]


def student_chunk(states, head_t, first, rows, owners, tokens):
    depth = head_t.shape[1]
    width = tokens // owners
    tile = tile_of(rows, TILE)
    base = first // tile
    outs = [pl.BlockSpec((tile, width), lambda i: (i, 0))] * owners
    shapes = [jax.ShapeDtypeStruct((rows, width), F32)] * owners
    places = None
    if isinstance(states, tuple):
        places = tuple((a, at) for _, a, at in states[1])
        args = [states[0]] + [x for x, _, _ in states[1]]
        specs = [pl.BlockSpec(memory_space=pltpu.SMEM)] + [whole(x.shape) for x in args[1:]]
        outs = outs + [whole((tokens, depth)), whole((depth, tokens))]
        shapes = shapes + [
            jax.ShapeDtypeStruct((tokens, depth), BF16),
            jax.ShapeDtypeStruct((depth, tokens), BF16),
        ]
    else:
        args, specs = [states], [whole((depth, tokens))]
    return pl.pallas_call(
        functools.partial(student_body, owners, places),
        grid=(rows // tile,),
        in_specs=specs + [pl.BlockSpec((tile, depth), lambda i: (i + base, 0))],
        out_specs=outs,
        out_shape=shapes,
        compiler_params=params(28),
        cost_estimate=cost(
            2 * rows * tokens * depth, 2 * rows * depth + 2 * tokens * depth + 4 * rows * tokens
        ),
        name="student_chunk",
    )(*args, head_t)


def merge(refs, shifts, width):
    rows = []
    for ref, shift in zip(refs, shifts):
        x = ref[...]
        if shift:
            cut = [x[:, at : at + width] for at in range(0, x.shape[1], width)]
            x = jnp.concatenate([cut[w ^ shift] for w in range(len(cut))], axis=1)
        rows.append(x)
    top_s = functools.reduce(jnp.maximum, [x[0:1] for x in rows])
    top_t = functools.reduce(jnp.maximum, [x[1:2] for x in rows])
    terms = []
    for x in rows:
        scale_s = jnp.exp(x[0:1] - top_s)
        scale_t = jnp.exp(x[1:2] - top_t)
        terms.append([x[2:3] * scale_s, x[3:4] * scale_t, x[4:5] * scale_t])
    while len(terms) > 1:
        terms = [
            [a + b for a, b in zip(left, right)] for left, right in zip(terms[::2], terms[1::2])
        ]
    return [top_s, top_t] + terms[0]


def merge_body(shifts, width, *refs):
    *in_refs, out_ref = refs
    out_ref[...] = jnp.zeros(out_ref.shape, F32)
    for row, value in enumerate(merge(in_refs, shifts, width)):
        out_ref[row : row + 1] = value


def finish_body(shifts, width, *refs):
    *in_refs, mask_ref, coef_ref, kl_ref = refs
    top_s, top_t, sum_s, sum_t, cross = merge(in_refs, shifts, width)
    mask = mask_ref[...]
    coef_ref[...] = jnp.zeros(coef_ref.shape, F32)
    coef_ref[0:1] = top_s
    coef_ref[1:2] = top_t
    coef_ref[2:3] = mask / sum_s
    coef_ref[3:4] = mask / sum_t
    kl_ref[...] = mask * (cross / sum_t - top_t - jnp.log(sum_t) + top_s + jnp.log(sum_s))


def merge_call(values, shifts, width, mask=None):
    shape = values[0].shape
    out = jax.ShapeDtypeStruct(shape, F32)
    small = pltpu.CompilerParams(vmem_limit_bytes=2 * MIB)
    guess = cost(1 << 20, 1 << 16)
    if mask is None:
        return pl.pallas_call(
            functools.partial(merge_body, shifts, width),
            out_shape=out,
            compiler_params=small,
            cost_estimate=guess,
            name="merge_totals",
        )(*values)
    kl = jax.ShapeDtypeStruct((1, shape[1]), F32)
    return pl.pallas_call(
        functools.partial(finish_body, shifts, width),
        out_shape=(out, kl),
        compiler_params=small,
        cost_estimate=guess,
        name="finish_totals",
    )(*values, mask)


def grads_body(count, *refs):
    parts, teacher_refs = refs[:count], refs[count:-2]
    coef_ref, out_ref = refs[-2:]
    width = out_ref.shape[1] // len(teacher_refs)
    for w, teacher_ref in enumerate(teacher_refs):
        lanes = slice(w * width, (w + 1) * width)
        coef = coef_ref[:, lanes]
        student = parts[0][:, lanes]
        for part in parts[1:]:
            student = student + part[:, lanes]
        target = teacher_ref[...].astype(F32)
        out_ref[:, lanes] = (
            jnp.exp(student - coef[0:1]) * coef[2:3] - jnp.exp(target - coef[1:2]) * coef[3:4]
        ).astype(BF16)


def grads_chunk(parts, teachers, coef, first):
    rows, width = parts[0].shape
    tile = tile_of(rows, 2 * TILE)
    return pl.pallas_call(
        functools.partial(grads_body, len(parts)),
        grid=(rows // tile,),
        in_specs=chunk_specs([*parts, *teachers], tile, first, teachers[0].shape[0])
        + [whole(coef.shape)],
        out_specs=pl.BlockSpec((tile, width), lambda i: (i, 0)),
        out_shape=jax.ShapeDtypeStruct((rows, width), BF16),
        compiler_params=params(20),
        cost_estimate=cost(
            8 * rows * width, (4 * len(parts) + 4) * rows * width, 2 * rows * width
        ),
        name="logit_grads_chunk",
    )(*parts, *teachers, coef)


def chunk_specs(arrays, tile, first, total):
    return [
        pl.BlockSpec(
            (tile, x.shape[1]),
            functools.partial(lambda base, i: (i + base, 0), first // tile if x.shape[0] == total else 0),
        )
        for x in arrays
    ]


def hidden_body(count, owners, has_acc, emit, last, *refs):
    grads_refs, head_ref, *rest = (refs[:count], *refs[count:])
    before_ref = rest.pop(0) if has_acc else None
    if emit:
        turned_ref = rest.pop(0)

        @pl.when(pl.program_id(0) == 0)
        def _():
            for k, ref in enumerate(grads_refs):
                width = ref.shape[1]
                turned_ref[k * width : (k + 1) * width] = ref[...].T

    else:
        turned_ref = grads_refs[0]
    total = jnp.dot(turned_ref[...], head_ref[...], preferred_element_type=F32)
    if has_acc:
        total = total + before_ref[...]
    if not last:
        rest[0][...] = total
        return
    shard = total.shape[0] // (owners * len(rest))
    for k in range(owners):
        for w, out_ref in enumerate(rest):
            at = (k * len(rest) + w) * shard
            out_ref[k * shard : (k + 1) * shard] = total[at : at + shard].astype(BF16)


def hidden_chunk(grads, head_t, first, rows, owners, waves, tile, tiles, emit, before, last):
    width = COLUMNS if head_t.shape[1] % COLUMNS == 0 else 128
    base = first // rows
    tokens = sum(g.shape[1] for g in grads) if emit else grads[0].shape[0]
    block = pl.BlockSpec((tokens, width), lambda i: (0, i))
    size = tiles * width
    pieces = waves if last else 1
    out_specs = [pl.BlockSpec((tokens // pieces, width), lambda i: (0, i))] * pieces
    out_shape = [jax.ShapeDtypeStruct((tokens // pieces, size), BF16 if last else F32)] * pieces
    if emit:
        out_specs = [whole((tokens, rows))] + out_specs
        out_shape = [jax.ShapeDtypeStruct((tokens, rows), BF16)] + out_shape
    has_acc = before is not None
    return pl.pallas_call(
        functools.partial(hidden_body, len(grads), owners, has_acc, emit, last),
        grid=(tiles,),
        in_specs=[whole(g.shape) for g in grads]
        + [pl.BlockSpec((rows, width), lambda i: (base, i + tile))]
        + [block] * has_acc,
        out_specs=out_specs,
        out_shape=out_shape,
        compiler_params=params(32),
        cost_estimate=cost(2 * rows * tokens * size, 2 * rows * (size + tokens)),
        name="grad_hidden_chunk",
    )(*grads, head_t, *([before] if has_acc else []))


def head_body(count, hidden_ref, *refs):
    grads = jnp.concatenate([ref[...] for ref in refs[:count]], axis=1)
    out_ref, flag_ref = refs[-2:]

    @pl.when(pl.program_id(0) == 0)
    def _():
        flag_ref[...] = jnp.zeros(flag_ref.shape, F32)

    for at in range(0, out_ref.shape[1], COLUMNS):
        lanes = slice(at, min(at + COLUMNS, out_ref.shape[1]))
        out_ref[:, lanes] = jnp.dot(
            grads, hidden_ref[:, lanes], preferred_element_type=F32
        ).astype(BF16)


def head_chunk(hidden, grads, first, total, before):
    rows = grads[0].shape[0]
    tokens, depth = hidden.shape
    tile = tile_of(rows, TILE)
    base = first // tile
    specs = [whole(hidden.shape)] + chunk_specs(grads, tile, first, total)
    extra, aliases = [], {}
    if before is not None:
        specs.append(pl.BlockSpec(memory_space=pl.ANY))
        extra, aliases = [before], {1 + len(grads): 0}
    return pl.pallas_call(
        functools.partial(head_body, len(grads)),
        grid=(rows // tile,),
        in_specs=specs,
        out_specs=[pl.BlockSpec((tile, depth), lambda i: (i + base, 0)), whole((8, 128))],
        out_shape=[
            jax.ShapeDtypeStruct((total, depth), BF16),
            jax.ShapeDtypeStruct((8, 128), F32),
        ],
        input_output_aliases=aliases,
        compiler_params=params(24),
        cost_estimate=cost(
            2 * rows * tokens * depth, 2 * rows * depth + 2 * tokens * depth + 2 * rows * tokens
        ),
        name="grad_head_chunk",
    )(hidden, *grads, *extra)


def swap(x, axis, k):
    n = lax.axis_size(axis)
    return lax.ppermute(x, axis, [(i, i ^ k) for i in range(n)])


def merge_over(totals, axis, waves, mask=None):
    n = lax.axis_size(axis)
    width = totals.shape[1] // waves
    step = 1
    while step < n:
        span = min(4, n // step)
        values = [totals] + [swap(totals, axis, k * step) for k in range(1, span)]
        shifts = tuple(k * step % waves if axis == "dp" else 0 for k in range(span))
        step *= span
        totals = merge_call(values, shifts, width, mask if step == n else None)
    return totals


def rows_at(x, index, size):
    return lax.dynamic_slice_in_dim(x, index * size, size)


class Reduction:
    def __init__(self, partial, shard, own):
        self.partial, self.shard, self.own = partial, shard, own
        self.owners = lax.axis_size("mp")
        self.waves = lax.axis_size("dp") // self.owners

    def over_inner(self, flag):
        total = self.partial[0].astype(F32)
        for w in range(1, self.waves):
            total += tie(swap(self.partial[w], "dp", w), flag).astype(F32)
        self.total = total
        return total

    def over_outer(self, flag):
        total = rows_at(self.total, self.own, self.shard)
        for a in range(1, self.owners):
            sent = rows_at(self.total, self.own ^ a, self.shard).astype(BF16)
            total += tie(swap(sent, "dp", a * self.waves), flag).astype(F32)
        self.total = total
        return total

    def scatter_vocab(self, flag):
        n = lax.axis_size("vocab")
        if n > 4 or self.shard % (8 * n):
            self.block = lax.psum(self.total, "vocab")
            return self.block
        mine, size = lax.axis_index("vocab"), self.shard // n
        block = rows_at(self.total, mine, size)
        for c in range(1, n):
            sent = rows_at(self.total, mine ^ c, size).astype(BF16)
            block += tie(swap(sent, "vocab", c), flag).astype(F32)
        self.block = block.astype(BF16)
        return self.block

    def gather_vocab(self, flag):
        if self.block.shape[0] == self.shard:
            return self.block
        n = lax.axis_size("vocab")
        mine, size = lax.axis_index("vocab"), self.shard // n
        result = jnp.zeros(self.total.shape, F32)
        for c in range(n):
            piece = tie(swap(self.block, "vocab", c), flag) if c else self.block
            result = lax.dynamic_update_slice_in_dim(
                result, piece.astype(F32), (mine ^ c) * size, 0
            )
        return result


def tie(x, *after):
    return lax.optimization_barrier((x, *after))[0]


def per_device(hidden, head_weight, teacher_logits, response_start):
    n_dp, n_mp = lax.axis_size("dp"), lax.axis_size("mp")
    waves = n_dp // n_mp
    shard, depth = hidden.shape
    own_rows, columns = teacher_logits.shape
    mp = lax.axis_index("mp")
    dp = lax.axis_index("dp")
    outer, inner = dp // waves, dp % waves
    own = outer ^ mp
    head_t = head_weight.T
    teacher_t = teacher_logits.T

    def in_wave(x, w):
        return lax.dynamic_slice_in_dim(x, (inner ^ w) * shard, shard, axis=1)

    positions = mp * own_rows + jnp.concatenate(
        [(inner ^ w) * shard + jnp.arange(shard, dtype=jnp.int32) for w in range(waves)]
    )
    sequence = positions // LEN
    seq_ids = jnp.arange(response_start.shape[0], dtype=jnp.int32)
    starts = jnp.sum(
        jnp.where(sequence[:, None] == seq_ids[None, :], response_start[None, :], 0), axis=1
    )
    mask = (positions % LEN >= starts).astype(F32)[None, :]
    teachers = [in_wave(teacher_t, w) for w in range(waves)]

    near = {k: swap(hidden, "dp", k) for k in range(1, n_dp) if k < waves or k % waves == 0}
    pieces = [(tie(hidden, *teachers), 0, 0)]
    for k in range(1, n_dp):
        a, w = k // waves, k % waves
        if k in near:
            pieces.append((near[k], a, w * shard))
        else:
            half = shard // 2
            pieces.append((swap(near[a * waves][:half], "dp", w), a, w * shard))
            pieces.append((swap(near[w][half:], "dp", a * waves), a, w * shard + half))

    chunks = divide(columns, 3, 16)
    rows = columns // chunks
    firsts = [c * rows for c in range(chunks)]
    sub = 8 if columns % 8 == 0 else 1

    def exchanged(outs):
        return [outs[0]] + [swap(outs[k], "mp", k) for k in range(1, n_mp)]

    parts = []
    states = (own.astype(jnp.int32).reshape(1), pieces)
    for first in firsts:
        outs = student_chunk(states, head_t, first, rows, n_mp, n_dp * shard)
        if len(outs) > n_mp:
            ordered, states = outs[n_mp:]
        parts.append(exchanged(outs[:n_mp]))
    totals = start_totals(sub, own_rows)
    for c, first in enumerate(firsts):
        totals = totals_chunk(parts[c], teachers, first, totals, c == chunks - 1)
    totals = merge_over(totals, "dp", waves)
    coef, kl = merge_over(totals, "vocab", waves, mask)
    token_kl = jnp.zeros((1, own_rows), F32)
    for w in range(waves):
        token_kl = lax.dynamic_update_slice_in_dim(
            token_kl, kl[:, w * shard : (w + 1) * shard], (inner ^ w) * shard, 1
        )

    all_grads = []
    for c, first in enumerate(firsts):
        all_grads.append(exchanged([grads_chunk(parts[c], teachers, coef, first)] * n_mp))

    tiles = depth // (COLUMNS if depth % COLUMNS == 0 else 128)
    split = (tiles + 1) // 2
    reductions = []
    turned = [None] * chunks
    for at, count in ((0, split), (split, tiles - split)):
        acc = None
        for c, first in enumerate(firsts):
            inputs = all_grads[c] if at == 0 else [turned[c]]
            outs = hidden_chunk(
                inputs, head_t, first, rows, n_mp, waves, at, count, at == 0, acc, c == chunks - 1
            )
            if at == 0:
                turned[c], *outs = outs
            acc = outs[0]
        turned[0] = tie(turned[0], *outs)
        reductions.append(Reduction(outs, shard, own))
    results = [reductions[0].over_inner(reductions[-1].partial[0])]
    plan = [
        lambda flag: [reductions[0].over_outer(flag)]
        + [r.over_inner(flag) for r in reductions[1:]],
        lambda flag: [reductions[0].scatter_vocab(flag)]
        + [r.over_outer(flag) for r in reductions[1:]],
        lambda flag: [reductions[0].gather_vocab(flag)]
        + [r.scatter_vocab(flag) for r in reductions[1:]],
    ]
    grad_head = None
    for c, first in enumerate(firsts):
        grad_head, flag = head_chunk(
            tie(ordered, *results), all_grads[c], first, columns, grad_head
        )
        if plan:
            results = plan.pop(0)(flag)
    while plan:
        results = plan.pop(0)(flag)
    grad_hidden = jnp.concatenate(
        [results[0]] + [r.gather_vocab(flag) for r in reductions[1:]], axis=1
    )
    return (token_kl.reshape(own_rows), grad_hidden, grad_head.T)


def solution(mesh):
    return jax.shard_map(
        per_device,
        mesh=mesh,
        in_specs=(P("dp", "mp"), P("mp", ("dp", "vocab")), P("mp", ("dp", "vocab")), P()),
        out_specs=(P("mp"), P("dp", "mp"), P("mp", ("dp", "vocab"))),
        check_vma=False,
    )
```

```python
import functools

import jax
import jax.numpy as jnp
from jax import lax
from jax.experimental import pallas as pl
from jax.experimental.pallas import tpu as pltpu
from jax.sharding import PartitionSpec as P

LEN = 256
F32 = jnp.float32
BF16 = jnp.bfloat16
MIB = 1 << 20
WEIGHT = 1 / 16
TILE = 528
ALL = 63
UNREAD = pl.BlockSpec(memory_space=pl.ANY)
SLICE = 48
COLUMNS = 256


def chunks_of(total, parts):
    if total % (16 * parts):
        parts = 1
    size = total // parts
    return [(c * size, size) for c in range(parts)]


def tile_of(rows, want):
    for size in range(min(want, rows) // 16 * 16, 0, -16):
        if rows % size == 0:
            return size
    return rows


def params(mib):
    return pltpu.CompilerParams(
        dimension_semantics=("arbitrary",), vmem_limit_bytes=mib * MIB
    )


def cost(flops, moved, exps=0):
    return pl.CostEstimate(
        flops=int(flops * WEIGHT),
        bytes_accessed=int(moved * WEIGHT),
        transcendentals=int(exps * WEIGHT),
    )


def whole(shape):
    return pl.BlockSpec(shape, lambda i: (0,) * len(shape))


def fold(op, x, sub):
    if sub == 1:
        return (jnp.max if op is jnp.maximum else jnp.sum)(x, axis=0, keepdims=True)
    x = x.reshape(x.shape[0] // sub, sub, x.shape[1])
    while x.shape[0] > 1:
        half = x.shape[0] // 2
        rest = x[2 * half :]
        x = op(x[:half], x[half : 2 * half])
        if rest.shape[0]:
            x = jnp.concatenate([x, rest], axis=0)
    return x[0]


def spread(op, x, row, sub):
    if sub == 1:
        return op(x, row)
    rows, width = x.shape
    return op(x.reshape(rows // sub, sub, width), row[None]).reshape(rows, width)


def add_totals(parts, teacher_refs, state_ref, sub):
    total = teacher_refs[0].shape[0]
    size = tile_of(total, SLICE)
    slices = [slice(at, at + size) for at in range(0, total, size)]

    def load(rows):
        student = parts[0][rows]
        for part in parts[1:]:
            student = student + part[rows]
        target = jnp.concatenate([ref[rows] for ref in teacher_refs], axis=1).astype(F32)
        return student, target

    old = [state_ref[sub * r : sub * (r + 1)] for r in range(5)]
    top_s, top_t = old[:2]
    for rows in slices:
        student, target = load(rows)
        top_s = jnp.maximum(top_s, fold(jnp.maximum, student, sub))
        top_t = jnp.maximum(top_t, fold(jnp.maximum, target, sub))
    scale_s = jnp.exp(old[0] - top_s)
    scale_t = jnp.exp(old[1] - top_t)
    sum_s, sum_t, cross = old[2] * scale_s, old[3] * scale_t, old[4] * scale_t
    for rows in slices:
        student, target = load(rows)
        exp_s = jnp.exp(spread(jnp.subtract, student, top_s, sub))
        exp_t = jnp.exp(spread(jnp.subtract, target, top_t, sub))
        sum_s += fold(jnp.add, exp_s, sub)
        sum_t += fold(jnp.add, exp_t, sub)
        cross += fold(jnp.add, exp_t * (target - student), sub)
    for r, value in enumerate([top_s, top_t, sum_s, sum_t, cross]):
        state_ref[sub * r : sub * (r + 1)] = value


def merge_classes(state_ref, sub):
    rows = [state_ref[sub * r : sub * (r + 1)] for r in range(5)]
    top_s = jnp.max(rows[0], axis=0, keepdims=True)
    top_t = jnp.max(rows[1], axis=0, keepdims=True)
    scale_s = jnp.exp(rows[0] - top_s)
    scale_t = jnp.exp(rows[1] - top_t)
    return [
        top_s,
        top_t,
        jnp.sum(rows[2] * scale_s, axis=0, keepdims=True),
        jnp.sum(rows[3] * scale_t, axis=0, keepdims=True),
        jnp.sum(rows[4] * scale_t, axis=0, keepdims=True),
    ]


def start_totals(sub, width):
    return jnp.concatenate(
        [jnp.full((2 * sub, width), -jnp.inf, F32), jnp.zeros((3 * sub, width), F32)]
    )


def totals_body(count, waves, sub, last, *refs):
    parts, teacher_refs = refs[:count], refs[count : count + waves]
    before_ref, out_ref, state_ref = refs[count + waves :]
    step = pl.program_id(0)

    @pl.when(step == 0)
    def _():
        state_ref[...] = before_ref[...]

    add_totals(parts, teacher_refs, state_ref, sub)

    @pl.when(step == pl.num_programs(0) - 1)
    def _():
        if last:
            out_ref[...] = jnp.zeros(out_ref.shape, F32)
            for r, value in enumerate(merge_classes(state_ref, sub)):
                out_ref[r : r + 1] = value
        else:
            out_ref[...] = state_ref[...]


def row_blocks(arrays, tile, skip=0):
    return [pl.BlockSpec((tile, x.shape[1]), lambda i: (i + skip, 0)) for x in arrays]


def totals_chunk(parts, teachers, before, last):
    rows, width = parts[0].shape
    sub = before.shape[0] // 5
    tile = tile_of(rows, TILE)
    out = (8 if last else 5 * sub, width)
    return pl.pallas_call(
        functools.partial(totals_body, len(parts), len(teachers), sub, last),
        grid=(rows // tile,),
        in_specs=row_blocks([*parts, *teachers], tile) + [whole(before.shape)],
        out_specs=whole(out),
        out_shape=jax.ShapeDtypeStruct(out, F32),
        scratch_shapes=[pltpu.VMEM((5 * sub, width), F32)],
        compiler_params=params(ALL),
        cost_estimate=cost(
            12 * rows * width, (4 * len(parts) + 2) * rows * width, 2 * rows * width
        ),
        name="totals_chunk",
    )(*parts, *teachers, before)


def student_body(owners, places, after, *refs):
    refs = list(refs[after:])
    if places is not None:
        own_ref = refs.pop(0)
        piece_refs = [refs.pop(0) for _ in places]
        turned_ref, ordered_ref = refs.pop(), refs.pop()

        for own in range(owners):

            @pl.when((pl.program_id(0) == 0) & (own_ref[0] == own))
            def _():
                for (a, at), ref in zip(places, piece_refs):
                    start = (own ^ a) * (ordered_ref.shape[0] // owners) + at
                    ordered_ref[start : start + ref.shape[0]] = ref[...]

        @pl.when(pl.program_id(0) == 0)
        def _():
            turned_ref[...] = ordered_ref[...].T

    else:
        turned_ref = refs.pop(0)
    head_ref, *out_refs = refs
    width = out_refs[0].shape[1]
    for k, out_ref in enumerate(out_refs):
        out_ref[...] = jnp.dot(
            head_ref[...], turned_ref[:, k * width : (k + 1) * width], preferred_element_type=F32
        )


def student_chunk(states, head_t, first, rows, owners, tokens, after):
    depth = head_t.shape[1]
    width = tokens // owners
    tile = tile_of(rows, TILE)
    base = first // tile
    outs = [pl.BlockSpec((tile, width), lambda i: (i, 0))] * owners
    shapes = [jax.ShapeDtypeStruct((rows, width), F32)] * owners
    places = None
    if isinstance(states, tuple):
        places = tuple((a, at) for _, a, at in states[1])
        args = [states[0]] + [x for x, _, _ in states[1]]
        specs = [pl.BlockSpec(memory_space=pltpu.SMEM)] + [whole(x.shape) for x in args[1:]]
        outs = outs + [whole((tokens, depth)), whole((depth, tokens))]
        shapes = shapes + [
            jax.ShapeDtypeStruct((tokens, depth), BF16),
            jax.ShapeDtypeStruct((depth, tokens), BF16),
        ]
    else:
        args, specs = [states], [whole((depth, tokens))]
    return pl.pallas_call(
        functools.partial(student_body, owners, places, len(after)),
        grid=(rows // tile,),
        in_specs=[UNREAD] * len(after)
        + specs
        + [pl.BlockSpec((tile, depth), lambda i: (i + base, 0))],
        out_specs=outs,
        out_shape=shapes,
        compiler_params=params(ALL),
        cost_estimate=cost(
            2 * rows * tokens * depth, 2 * rows * depth + 2 * tokens * depth + 4 * rows * tokens
        ),
        name="student_chunk",
    )(*after, *args, head_t)


def merge(refs, shifts, width):
    rows = []
    for ref, shift in zip(refs, shifts):
        x = ref[...]
        if shift:
            cut = [x[:, at : at + width] for at in range(0, x.shape[1], width)]
            x = jnp.concatenate([cut[w ^ shift] for w in range(len(cut))], axis=1)
        rows.append(x)
    top_s = functools.reduce(jnp.maximum, [x[0:1] for x in rows])
    top_t = functools.reduce(jnp.maximum, [x[1:2] for x in rows])
    terms = []
    for x in rows:
        scale_s = jnp.exp(x[0:1] - top_s)
        scale_t = jnp.exp(x[1:2] - top_t)
        terms.append([x[2:3] * scale_s, x[3:4] * scale_t, x[4:5] * scale_t])
    while len(terms) > 1:
        terms = [
            [a + b for a, b in zip(left, right)] for left, right in zip(terms[::2], terms[1::2])
        ]
    return [top_s, top_t] + terms[0]


def merge_body(shifts, width, *refs):
    *in_refs, out_ref = refs
    out_ref[...] = jnp.zeros(out_ref.shape, F32)
    for row, value in enumerate(merge(in_refs, shifts, width)):
        out_ref[row : row + 1] = value


def finish_body(shifts, width, *refs):
    *in_refs, mask_ref, coef_ref, kl_ref = refs
    top_s, top_t, sum_s, sum_t, cross = merge(in_refs, shifts, width)
    mask = mask_ref[...]
    coef_ref[...] = jnp.zeros(coef_ref.shape, F32)
    coef_ref[0:1] = top_s
    coef_ref[1:2] = top_t
    coef_ref[2:3] = mask / sum_s
    coef_ref[3:4] = mask / sum_t
    kl_ref[...] = mask * (cross / sum_t - top_t - jnp.log(sum_t) + top_s + jnp.log(sum_s))


def merge_call(values, shifts, width, mask=None):
    shape = values[0].shape
    out = jax.ShapeDtypeStruct(shape, F32)
    small = pltpu.CompilerParams(vmem_limit_bytes=2 * MIB)
    guess = cost(1 << 20, 1 << 16)
    if mask is None:
        return pl.pallas_call(
            functools.partial(merge_body, shifts, width),
            out_shape=out,
            compiler_params=small,
            cost_estimate=guess,
            name="merge_totals",
        )(*values)
    kl = jax.ShapeDtypeStruct((1, shape[1]), F32)
    return pl.pallas_call(
        functools.partial(finish_body, shifts, width),
        out_shape=(out, kl),
        compiler_params=small,
        cost_estimate=guess,
        name="finish_totals",
    )(*values, mask)


def grads_body(count, *refs):
    parts, teacher_refs = refs[:count], refs[count:-2]
    coef_ref, out_ref = refs[-2:]
    width = out_ref.shape[1] // len(teacher_refs)
    for w, teacher_ref in enumerate(teacher_refs):
        lanes = slice(w * width, (w + 1) * width)
        coef = coef_ref[:, lanes]
        student = parts[0][:, lanes]
        for part in parts[1:]:
            student = student + part[:, lanes]
        target = teacher_ref[...].astype(F32)
        out_ref[:, lanes] = (
            jnp.exp(student - coef[0:1]) * coef[2:3] - jnp.exp(target - coef[1:2]) * coef[3:4]
        ).astype(BF16)


def grads_chunk(parts, teachers, coef):
    rows, width = parts[0].shape
    tile = tile_of(rows, 2 * TILE)
    return pl.pallas_call(
        functools.partial(grads_body, len(parts)),
        grid=(rows // tile,),
        in_specs=row_blocks([*parts, *teachers], tile) + [whole(coef.shape)],
        out_specs=pl.BlockSpec((tile, width), lambda i: (i, 0)),
        out_shape=jax.ShapeDtypeStruct((rows, width), BF16),
        compiler_params=params(14),
        cost_estimate=cost(
            8 * rows * width, (4 * len(parts) + 4) * rows * width, 2 * rows * width
        ),
        name="logit_grads_chunk",
    )(*parts, *teachers, coef)


def hidden_body(count, after, has_acc, last, *refs):
    refs = refs[after:]
    grads_refs, head_ref, *rest = (refs[:count], *refs[count:])
    before_ref = rest.pop(0) if has_acc else None
    *out_refs, turned_ref = rest

    @pl.when(pl.program_id(0) == 0)
    def _():
        for k, ref in enumerate(grads_refs):
            width = ref.shape[1]
            turned_ref[k * width : (k + 1) * width] = ref[...].T

    total = jnp.dot(turned_ref[...], head_ref[...], preferred_element_type=F32)
    if has_acc:
        total = total + before_ref[...]
    if not last:
        out_refs[0][...] = total
        return
    waves = len(out_refs)
    shard = total.shape[0] // (count * waves)
    for k in range(count):
        for w, out_ref in enumerate(out_refs):
            at = (k * waves + w) * shard
            out_ref[k * shard : (k + 1) * shard] = total[at : at + shard].astype(BF16)


def hidden_chunk(grads, head_t, first, waves, tile, tiles, before, last, after):
    rows = grads[0].shape[0]
    width = COLUMNS if head_t.shape[1] % COLUMNS == 0 else 128
    base = first // rows
    tokens = sum(g.shape[1] for g in grads)
    size = tiles * width
    pieces = waves if last else 1
    block = lambda count: pl.BlockSpec((count, width), lambda i: (0, i))
    has_acc = before is not None
    return pl.pallas_call(
        functools.partial(hidden_body, len(grads), len(after), has_acc, last),
        grid=(tiles,),
        in_specs=[UNREAD] * len(after)
        + [whole(g.shape) for g in grads]
        + [pl.BlockSpec((rows, width), lambda i: (base, i + tile))]
        + [block(tokens)] * has_acc,
        out_specs=[block(tokens // pieces)] * pieces,
        out_shape=[jax.ShapeDtypeStruct((tokens // pieces, size), BF16 if last else F32)] * pieces,
        scratch_shapes=[pltpu.VMEM((tokens, rows), BF16)],
        compiler_params=params(32),
        cost_estimate=cost(2 * rows * tokens * size, 2 * rows * (size + tokens)),
        name="grad_hidden_chunk",
    )(*after, *grads, head_t, *([before] if has_acc else []))


def head_body(count, after, *refs):
    hidden_ref, *refs = refs[after:]
    grads = jnp.concatenate([ref[...] for ref in refs[:count]], axis=1)
    out_ref, flag_ref = refs[-2:]

    @pl.when(pl.program_id(0) == 0)
    def _():
        flag_ref[...] = jnp.zeros(flag_ref.shape, F32)

    for at in range(0, out_ref.shape[1], COLUMNS):
        lanes = slice(at, min(at + COLUMNS, out_ref.shape[1]))
        out_ref[:, lanes] = jnp.dot(
            grads, hidden_ref[:, lanes], preferred_element_type=F32
        ).astype(BF16)


def head_chunk(hidden, grads, first, skip, rows, total, before, after):
    tokens, depth = hidden.shape
    tile = tile_of(rows, TILE)
    base = (first + skip) // tile
    specs = [UNREAD] * len(after) + [whole(hidden.shape)] + row_blocks(grads, tile, skip // tile)
    extra, aliases = [], {}
    if before is not None:
        specs.append(UNREAD)
        extra, aliases = [before], {len(after) + 1 + len(grads): 0}
    return pl.pallas_call(
        functools.partial(head_body, len(grads), len(after)),
        grid=(rows // tile,),
        in_specs=specs,
        out_specs=[pl.BlockSpec((tile, depth), lambda i: (i + base, 0)), whole((8, 128))],
        out_shape=[
            jax.ShapeDtypeStruct((total, depth), BF16),
            jax.ShapeDtypeStruct((8, 128), F32),
        ],
        input_output_aliases=aliases,
        compiler_params=params(24),
        cost_estimate=cost(
            2 * rows * tokens * depth, 2 * rows * depth + 2 * tokens * depth + 2 * rows * tokens
        ),
        name="grad_head_chunk",
    )(*after, hidden, *grads, *extra)


def swap(x, axis, k):
    n = lax.axis_size(axis)
    return lax.ppermute(x, axis, [(i, i ^ k) for i in range(n)])


def merge_over(totals, axis, waves, mask=None):
    n = lax.axis_size(axis)
    width = totals.shape[1] // waves
    step = 1
    while step < n:
        span = min(4, n // step)
        values = [totals] + [swap(totals, axis, k * step) for k in range(1, span)]
        shifts = tuple(k * step % waves if axis == "dp" else 0 for k in range(span))
        step *= span
        totals = merge_call(values, shifts, width, mask if step == n else None)
    return totals


def rows_at(x, index, size):
    return lax.dynamic_slice_in_dim(x, index * size, size)


class Reduction:
    def __init__(self, partial, shard, own):
        self.partial, self.shard, self.own = partial, shard, own
        self.owners = lax.axis_size("mp")
        self.waves = lax.axis_size("dp") // self.owners

    def over_inner(self, flag):
        total = self.partial[0].astype(F32)
        for w in range(1, self.waves):
            total += late(swap(self.partial[w], "dp", w), flag)
        self.total = total
        return total

    def over_outer(self, flag):
        total = rows_at(self.total, self.own, self.shard)
        for a in range(1, self.owners):
            sent = rows_at(self.total, self.own ^ a, self.shard).astype(BF16)
            total += late(swap(sent, "dp", a * self.waves), flag)
        self.total = total
        return total

    def over_vocab(self, step, flag):
        n = lax.axis_size("vocab")
        if n > 4:
            if step == 1:
                self.total = lax.psum(self.total, "vocab")
        elif step < n:
            sent = self.total.astype(BF16)
            self.total = sent.astype(F32) + late(swap(sent, "vocab", step), flag)
        return self.total


def late(x, flag):
    x = x.astype(F32)
    return x if flag is None else x + flag[0, 0]


def per_device(hidden, head_weight, teacher_logits, response_start):
    n_dp, n_mp = lax.axis_size("dp"), lax.axis_size("mp")
    waves = n_dp // n_mp
    shard, depth = hidden.shape
    own_rows, columns = teacher_logits.shape
    mp = lax.axis_index("mp")
    dp = lax.axis_index("dp")
    outer, inner = dp // waves, dp % waves
    own = outer ^ mp
    head_t = head_weight.T
    teacher_t = teacher_logits.T

    positions = mp * own_rows + jnp.concatenate(
        [(inner ^ w) * shard + jnp.arange(shard, dtype=jnp.int32) for w in range(waves)]
    )
    sequence = positions // LEN
    seq_ids = jnp.arange(response_start.shape[0], dtype=jnp.int32)
    starts = jnp.sum(
        jnp.where(sequence[:, None] == seq_ids[None, :], response_start[None, :], 0), axis=1
    )
    mask = (positions % LEN >= starts).astype(F32)[None, :]
    chunks = chunks_of(columns, 3)
    teachers = [
        [
            lax.dynamic_slice(teacher_t, (first, (inner ^ w) * shard), (rows, shard))
            for w in range(waves)
        ]
        for first, rows in chunks
    ]

    near = {k: swap(hidden, "dp", k) for k in range(1, n_dp) if k < waves or k % waves == 0}
    pieces = [(hidden, 0, 0)]
    for k in range(1, n_dp):
        a, w = k // waves, k % waves
        if k in near:
            pieces.append((near[k], a, w * shard))
        else:
            half = shard // 2
            pieces.append((swap(near[a * waves][:half], "dp", w), a, w * shard))
            pieces.append((swap(near[w][half:], "dp", a * waves), a, w * shard + half))

    sub = 8 if columns % 8 == 0 else 1

    def exchanged(outs):
        return [outs[0]] + [swap(outs[k], "mp", k) for k in range(1, n_mp)]

    parts = []
    states = (own.astype(jnp.int32).reshape(1), pieces)
    for first, rows in chunks:
        after = [] if first else [x for chunk in teachers for x in chunk]
        outs = student_chunk(states, head_t, first, rows, n_mp, n_dp * shard, after)
        if len(outs) > n_mp:
            ordered, states = outs[n_mp:]
        parts.append(exchanged(outs[:n_mp]))
    totals = start_totals(sub, own_rows)
    for c in range(len(chunks)):
        totals = totals_chunk(parts[c], teachers[c], totals, c == len(chunks) - 1)
    totals = merge_over(totals, "dp", waves)
    coef, kl = merge_over(totals, "vocab", waves, mask)
    token_kl = jnp.zeros((1, own_rows), F32)
    for w in range(waves):
        token_kl = lax.dynamic_update_slice_in_dim(
            token_kl, kl[:, w * shard : (w + 1) * shard], (inner ^ w) * shard, 1
        )

    all_grads = []
    for c in range(len(chunks)):
        all_grads.append(exchanged([grads_chunk(parts[c], teachers[c], coef)] * n_mp))

    tiles = depth // (COLUMNS if depth % COLUMNS == 0 else 128)
    split = (tiles + 1) // 2
    reductions = []
    outs = []
    for at, count in ((0, split), (split, tiles - split)):
        acc, after = None, outs
        for c, (first, rows) in enumerate(chunks):
            last = c == len(chunks) - 1
            outs = hidden_chunk(
                all_grads[c], head_t, first, waves, at, count, acc, last, after
            )
            acc, after = outs[0], []
        reductions.append(Reduction(outs, shard, own))

    one, two = reductions
    results = [one.over_inner(None)]
    plan = [
        lambda flag: [one.over_outer(flag), two.over_inner(flag)],
        lambda flag: [one.over_vocab(1, flag), two.over_outer(flag)],
        lambda flag: [one.over_vocab(2, flag), two.over_vocab(1, flag)],
        lambda flag: [one.total, two.over_vocab(2, flag)],
    ]
    calls = [(c, 0, rows) for c, (_, rows) in enumerate(chunks)]
    if calls[-1][2] % (2 * TILE) == 0:
        c, _, rows = calls.pop()
        calls += [(c, 0, rows // 2), (c, rows // 2, rows // 2)]
    grad_head = None
    for c, skip, rows in calls:
        grad_head, flag = head_chunk(
            ordered, all_grads[c], chunks[c][0], skip, rows, columns, grad_head, results
        )
        results = plan.pop(0)(flag)
    while plan:
        results = plan.pop(0)(flag)
    grad_hidden = jnp.concatenate(results, axis=1)
    return (token_kl.reshape(own_rows), grad_hidden, grad_head.T)


def solution(mesh):
    return jax.shard_map(
        per_device,
        mesh=mesh,
        in_specs=(P("dp", "mp"), P("mp", ("dp", "vocab")), P("mp", ("dp", "vocab")), P()),
        out_specs=(P("mp"), P("dp", "mp"), P("mp", ("dp", "vocab"))),
        check_vma=False,
    )
```

```python
import functools

import jax
import jax.numpy as jnp
from jax import lax
from jax.experimental import pallas as pl
from jax.experimental.pallas import tpu as pltpu
from jax.sharding import PartitionSpec as P

LEN = 256
F32 = jnp.float32
BF16 = jnp.bfloat16
MIB = 1 << 20
WEIGHT = 1 / 16
TILE = 528
ALL = 63
UNREAD = pl.BlockSpec(memory_space=pl.ANY)
COLUMNS = 256


def chunks_of(total, parts):
    if total % (16 * parts):
        parts = 1
    size = total // parts
    return [(c * size, size) for c in range(parts)]


def tile_of(rows, want):
    for size in range(min(want, rows) // 16 * 16, 0, -16):
        if rows % size == 0:
            return size
    return rows


def params(mib):
    return pltpu.CompilerParams(
        dimension_semantics=("arbitrary",), vmem_limit_bytes=mib * MIB
    )


def cost(flops, moved, exps=0):
    return pl.CostEstimate(
        flops=int(flops * WEIGHT),
        bytes_accessed=int(moved * WEIGHT),
        transcendentals=int(exps * WEIGHT),
    )


def whole(shape):
    return pl.BlockSpec(shape, lambda i: (0,) * len(shape))


def fold(op, x, sub):
    if sub == 1:
        return (jnp.max if op is jnp.maximum else jnp.sum)(x, axis=0, keepdims=True)
    x = x.reshape(x.shape[0] // sub, sub, x.shape[1])
    while x.shape[0] > 1:
        half = x.shape[0] // 2
        rest = x[2 * half :]
        x = op(x[:half], x[half : 2 * half])
        if rest.shape[0]:
            x = jnp.concatenate([x, rest], axis=0)
    return x[0]


def spread(op, x, row, sub):
    if sub == 1:
        return op(x, row)
    rows, width = x.shape
    return op(x.reshape(rows // sub, sub, width), row[None]).reshape(rows, width)


def add_totals(parts, teacher_refs, state_ref, sub):
    student = parts[0][...]
    for part in parts[1:]:
        student = student + part[...]
    target = jnp.concatenate([ref[...] for ref in teacher_refs], axis=1).astype(F32)
    old = [state_ref[sub * r : sub * (r + 1)] for r in range(5)]
    top_s = jnp.maximum(old[0], fold(jnp.maximum, student, sub))
    top_t = jnp.maximum(old[1], fold(jnp.maximum, target, sub))
    exp_s = jnp.exp(spread(jnp.subtract, student, top_s, sub))
    exp_t = jnp.exp(spread(jnp.subtract, target, top_t, sub))
    scale_s = jnp.exp(old[0] - top_s)
    scale_t = jnp.exp(old[1] - top_t)
    new = [
        top_s,
        top_t,
        old[2] * scale_s + fold(jnp.add, exp_s, sub),
        old[3] * scale_t + fold(jnp.add, exp_t, sub),
        old[4] * scale_t + fold(jnp.add, exp_t * (target - student), sub),
    ]
    for r, value in enumerate(new):
        state_ref[sub * r : sub * (r + 1)] = value


def merge_classes(state_ref, sub):
    rows = [state_ref[sub * r : sub * (r + 1)] for r in range(5)]
    top_s = jnp.max(rows[0], axis=0, keepdims=True)
    top_t = jnp.max(rows[1], axis=0, keepdims=True)
    scale_s = jnp.exp(rows[0] - top_s)
    scale_t = jnp.exp(rows[1] - top_t)
    return [
        top_s,
        top_t,
        jnp.sum(rows[2] * scale_s, axis=0, keepdims=True),
        jnp.sum(rows[3] * scale_t, axis=0, keepdims=True),
        jnp.sum(rows[4] * scale_t, axis=0, keepdims=True),
    ]


def start_totals(sub, width):
    return jnp.concatenate(
        [jnp.full((2 * sub, width), -jnp.inf, F32), jnp.zeros((3 * sub, width), F32)]
    )


def totals_body(count, waves, sub, last, *refs):
    parts, teacher_refs = refs[:count], refs[count : count + waves]
    before_ref, out_ref, state_ref = refs[count + waves :]
    step = pl.program_id(0)

    @pl.when(step == 0)
    def _():
        state_ref[...] = before_ref[...]

    add_totals(parts, teacher_refs, state_ref, sub)

    @pl.when(step == pl.num_programs(0) - 1)
    def _():
        if last:
            out_ref[...] = jnp.zeros(out_ref.shape, F32)
            for r, value in enumerate(merge_classes(state_ref, sub)):
                out_ref[r : r + 1] = value
        else:
            out_ref[...] = state_ref[...]


def row_blocks(arrays, tile, skip=0):
    return [pl.BlockSpec((tile, x.shape[1]), lambda i: (i + skip, 0)) for x in arrays]


def totals_chunk(parts, teachers, before, last):
    rows, width = parts[0].shape
    sub = before.shape[0] // 5
    tile = tile_of(rows, TILE)
    out = (8 if last else 5 * sub, width)
    return pl.pallas_call(
        functools.partial(totals_body, len(parts), len(teachers), sub, last),
        grid=(rows // tile,),
        in_specs=row_blocks([*parts, *teachers], tile) + [whole(before.shape)],
        out_specs=whole(out),
        out_shape=jax.ShapeDtypeStruct(out, F32),
        scratch_shapes=[pltpu.VMEM((5 * sub, width), F32)],
        compiler_params=params(12),
        cost_estimate=cost(
            12 * rows * width, (4 * len(parts) + 2) * rows * width, 2 * rows * width
        ),
        name="totals_chunk",
    )(*parts, *teachers, before)


def student_body(owners, places, after, *refs):
    refs = list(refs[after:])
    if places is not None:
        own_ref = refs.pop(0)
        piece_refs = [refs.pop(0) for _ in places]
        turned_ref, ordered_ref = refs.pop(), refs.pop()

        for own in range(owners):

            @pl.when((pl.program_id(0) == 0) & (own_ref[0] == own))
            def _():
                for (a, at), ref in zip(places, piece_refs):
                    start = (own ^ a) * (ordered_ref.shape[0] // owners) + at
                    ordered_ref[start : start + ref.shape[0]] = ref[...]

        @pl.when(pl.program_id(0) == 0)
        def _():
            turned_ref[...] = ordered_ref[...].T

    else:
        turned_ref = refs.pop(0)
    head_ref, *out_refs = refs
    width = out_refs[0].shape[1]
    full = jnp.dot(head_ref[...], turned_ref[...], preferred_element_type=F32)
    for k, out_ref in enumerate(out_refs):
        out_ref[...] = full[:, k * width : (k + 1) * width]


def student_chunk(states, head_t, first, rows, owners, tokens, after):
    depth = head_t.shape[1]
    width = tokens // owners
    tile = tile_of(rows, TILE)
    base = first // tile
    outs = [pl.BlockSpec((tile, width), lambda i: (i, 0))] * owners
    shapes = [jax.ShapeDtypeStruct((rows, width), F32)] * owners
    places = None
    if isinstance(states, tuple):
        places = tuple((a, at) for _, a, at in states[1])
        args = [states[0]] + [x for x, _, _ in states[1]]
        specs = [pl.BlockSpec(memory_space=pltpu.SMEM)] + [whole(x.shape) for x in args[1:]]
        outs = outs + [whole((tokens, depth)), whole((depth, tokens))]
        shapes = shapes + [
            jax.ShapeDtypeStruct((tokens, depth), BF16),
            jax.ShapeDtypeStruct((depth, tokens), BF16),
        ]
    else:
        args, specs = [states], [whole((depth, tokens))]
    return pl.pallas_call(
        functools.partial(student_body, owners, places, len(after)),
        grid=(rows // tile,),
        in_specs=[UNREAD] * len(after)
        + specs
        + [pl.BlockSpec((tile, depth), lambda i: (i + base, 0))],
        out_specs=outs,
        out_shape=shapes,
        compiler_params=params(ALL),
        cost_estimate=cost(
            2 * rows * tokens * depth, 2 * rows * depth + 2 * tokens * depth + 4 * rows * tokens
        ),
        name="student_chunk",
    )(*after, *args, head_t)


def merge(refs, shifts, width):
    rows = []
    for ref, shift in zip(refs, shifts):
        x = ref[...]
        if shift:
            cut = [x[:, at : at + width] for at in range(0, x.shape[1], width)]
            x = jnp.concatenate([cut[w ^ shift] for w in range(len(cut))], axis=1)
        rows.append(x)
    top_s = functools.reduce(jnp.maximum, [x[0:1] for x in rows])
    top_t = functools.reduce(jnp.maximum, [x[1:2] for x in rows])
    terms = []
    for x in rows:
        scale_s = jnp.exp(x[0:1] - top_s)
        scale_t = jnp.exp(x[1:2] - top_t)
        terms.append([x[2:3] * scale_s, x[3:4] * scale_t, x[4:5] * scale_t])
    while len(terms) > 1:
        terms = [
            [a + b for a, b in zip(left, right)] for left, right in zip(terms[::2], terms[1::2])
        ]
    return [top_s, top_t] + terms[0]


def merge_body(shifts, width, *refs):
    *in_refs, out_ref = refs
    out_ref[...] = jnp.zeros(out_ref.shape, F32)
    for row, value in enumerate(merge(in_refs, shifts, width)):
        out_ref[row : row + 1] = value


def finish_body(shifts, width, *refs):
    *in_refs, mask_ref, coef_ref, kl_ref = refs
    top_s, top_t, sum_s, sum_t, cross = merge(in_refs, shifts, width)
    mask = mask_ref[...]
    coef_ref[...] = jnp.zeros(coef_ref.shape, F32)
    coef_ref[0:1] = top_s
    coef_ref[1:2] = top_t
    coef_ref[2:3] = mask / sum_s
    coef_ref[3:4] = mask / sum_t
    kl_ref[...] = mask * (cross / sum_t - top_t - jnp.log(sum_t) + top_s + jnp.log(sum_s))


def merge_call(values, shifts, width, mask=None):
    shape = values[0].shape
    out = jax.ShapeDtypeStruct(shape, F32)
    small = pltpu.CompilerParams(vmem_limit_bytes=2 * MIB)
    guess = cost(1 << 20, 1 << 16)
    if mask is None:
        return pl.pallas_call(
            functools.partial(merge_body, shifts, width),
            out_shape=out,
            compiler_params=small,
            cost_estimate=guess,
            name="merge_totals",
        )(*values)
    kl = jax.ShapeDtypeStruct((1, shape[1]), F32)
    return pl.pallas_call(
        functools.partial(finish_body, shifts, width),
        out_shape=(out, kl),
        compiler_params=small,
        cost_estimate=guess,
        name="finish_totals",
    )(*values, mask)


def grads_body(count, *refs):
    parts, teacher_refs = refs[:count], refs[count:-2]
    coef_ref, out_ref = refs[-2:]
    width = out_ref.shape[1] // len(teacher_refs)
    for w, teacher_ref in enumerate(teacher_refs):
        lanes = slice(w * width, (w + 1) * width)
        coef = coef_ref[:, lanes]
        student = parts[0][:, lanes]
        for part in parts[1:]:
            student = student + part[:, lanes]
        target = teacher_ref[...].astype(F32)
        out_ref[:, lanes] = (
            jnp.exp(student - coef[0:1]) * coef[2:3] - jnp.exp(target - coef[1:2]) * coef[3:4]
        ).astype(BF16)


def grads_chunk(parts, teachers, coef):
    rows, width = parts[0].shape
    tile = tile_of(rows, 2 * TILE)
    return pl.pallas_call(
        functools.partial(grads_body, len(parts)),
        grid=(rows // tile,),
        in_specs=row_blocks([*parts, *teachers], tile) + [whole(coef.shape)],
        out_specs=pl.BlockSpec((tile, width), lambda i: (i, 0)),
        out_shape=jax.ShapeDtypeStruct((rows, width), BF16),
        compiler_params=params(14),
        cost_estimate=cost(
            8 * rows * width, (4 * len(parts) + 4) * rows * width, 2 * rows * width
        ),
        name="logit_grads_chunk",
    )(*parts, *teachers, coef)


def turn(grads_refs, turned_ref):
    for k, ref in enumerate(grads_refs):
        width = ref.shape[1]
        turned_ref[k * width : (k + 1) * width] = ref[...].T


def put_waves(total, owners, out_refs):
    waves = len(out_refs)
    shard = total.shape[0] // (owners * waves)
    for k in range(owners):
        for w, out_ref in enumerate(out_refs):
            at = (k * waves + w) * shard
            out_ref[k * shard : (k + 1) * shard] = total[at : at + shard].astype(BF16)


def hidden_body(count, has_acc, last, *refs):
    grads_refs, head_ref, *rest = (refs[:count], *refs[count:])
    before_ref = rest.pop(0) if has_acc else None
    *out_refs, turned_ref = rest

    @pl.when(pl.program_id(0) == 0)
    def _():
        turn(grads_refs, turned_ref)

    total = jnp.dot(turned_ref[...], head_ref[...], preferred_element_type=F32)
    if has_acc:
        total = total + before_ref[...]
    if last:
        *out_refs, flag_ref = out_refs
        flag_ref[...] = jnp.zeros(flag_ref.shape, F32)
        put_waves(total, count, out_refs)
    else:
        out_refs[0][...] = total


def hidden_width(depth):
    return COLUMNS if depth % COLUMNS == 0 else 128


def hidden_chunk(grads, head_t, first, waves, tiles, before, last):
    rows = grads[0].shape[0]
    width = hidden_width(head_t.shape[1])
    base = first // rows
    tokens = sum(g.shape[1] for g in grads)
    size = tiles * width
    pieces = waves if last else 1
    block = lambda count: pl.BlockSpec((count, width), lambda i: (0, i))
    has_acc = before is not None
    flag = jax.ShapeDtypeStruct((8, 128), F32)
    return pl.pallas_call(
        functools.partial(hidden_body, len(grads), has_acc, last),
        grid=(tiles,),
        in_specs=[whole(g.shape) for g in grads]
        + [pl.BlockSpec((rows, width), lambda i: (base, i))]
        + [block(tokens)] * has_acc,
        out_specs=[block(tokens // pieces)] * pieces + [whole(flag.shape)] * last,
        out_shape=[jax.ShapeDtypeStruct((tokens // pieces, size), BF16 if last else F32)] * pieces
        + [flag] * last,
        scratch_shapes=[pltpu.VMEM((tokens, rows), BF16)],
        compiler_params=params(30),
        cost_estimate=cost(2 * rows * tokens * size, 2 * rows * (size + tokens)),
        name="grad_hidden_chunk",
    )(*grads, head_t, *([before] if has_acc else []))


def hidden_rest_body(chunks, owners, *refs):
    grads_refs, head_ref, *out_refs = refs[1 : 1 + chunks * owners], *refs[1 + chunks * owners :]
    *out_refs, turned_ref, acc_ref = out_refs
    tile, chunk = pl.program_id(0), pl.program_id(1)
    for c in range(chunks):

        @pl.when((tile == 0) & (chunk == c))
        def _():
            turn(grads_refs[c * owners : (c + 1) * owners], turned_ref.at[c])

    term = jnp.dot(turned_ref[chunk], head_ref[...], preferred_element_type=F32)

    @pl.when(chunk == 0)
    def _():
        acc_ref[...] = term

    @pl.when(chunk > 0)
    def _():
        acc_ref[...] += term

    @pl.when(chunk == chunks - 1)
    def _():
        put_waves(acc_ref[...], owners, out_refs)


def hidden_rest(all_grads, head_t, waves, tile, tiles, flag):
    chunks, owners = len(all_grads), len(all_grads[0])
    grads = [g for chunk in all_grads for g in chunk]
    rows, per_owner = grads[0].shape
    tokens = owners * per_owner
    width = hidden_width(head_t.shape[1])
    size = tiles * width
    full = lambda shape: pl.BlockSpec(shape, lambda i, c: (0, 0))
    return pl.pallas_call(
        functools.partial(hidden_rest_body, chunks, owners),
        grid=(tiles, chunks),
        in_specs=[UNREAD]
        + [full(g.shape) for g in grads]
        + [pl.BlockSpec((rows, width), lambda i, c: (c, i + tile))],
        out_specs=[pl.BlockSpec((tokens // waves, width), lambda i, c: (0, i))] * waves,
        out_shape=[jax.ShapeDtypeStruct((tokens // waves, size), BF16)] * waves,
        scratch_shapes=[
            pltpu.VMEM((chunks, tokens, rows), BF16),
            pltpu.VMEM((tokens, width), F32),
        ],
        compiler_params=pltpu.CompilerParams(
            dimension_semantics=("arbitrary", "arbitrary"), vmem_limit_bytes=38 * MIB
        ),
        cost_estimate=cost(
            2 * chunks * rows * tokens * size, 2 * chunks * rows * (size + tokens)
        ),
        name="grad_hidden_rest",
    )(flag, *grads, head_t)


def head_body(count, after, *refs):
    hidden_ref, *refs = refs[after:]
    grads = jnp.concatenate([ref[...] for ref in refs[:count]], axis=1)
    out_ref, *flag_refs = refs[-3:]

    @pl.when(pl.program_id(0) == 0)
    def _():
        for ref in flag_refs:
            ref[...] = jnp.zeros(ref.shape, F32)

    for at in range(0, out_ref.shape[1], COLUMNS):
        lanes = slice(at, min(at + COLUMNS, out_ref.shape[1]))
        out_ref[:, lanes] = jnp.dot(
            grads, hidden_ref[:, lanes], preferred_element_type=F32
        ).astype(BF16)


def head_chunk(hidden, grads, first, skip, rows, total, before, after, widths):
    tokens, depth = hidden.shape
    tile = tile_of(rows, TILE)
    base = (first + skip) // tile
    specs = [UNREAD] * len(after) + [whole(hidden.shape)] + row_blocks(grads, tile, skip // tile)
    extra, aliases = [], {}
    if before is not None:
        specs.append(UNREAD)
        extra, aliases = [before], {len(after) + 1 + len(grads): 0}
    return pl.pallas_call(
        functools.partial(head_body, len(grads), len(after)),
        grid=(rows // tile,),
        in_specs=specs,
        out_specs=[pl.BlockSpec((tile, depth), lambda i: (i + base, 0))]
        + [whole((1, n)) for n in widths],
        out_shape=[jax.ShapeDtypeStruct((total, depth), BF16)]
        + [jax.ShapeDtypeStruct((1, n), F32) for n in widths],
        input_output_aliases=aliases,
        compiler_params=params(24),
        cost_estimate=cost(
            2 * rows * tokens * depth, 2 * rows * depth + 2 * tokens * depth + 2 * rows * tokens
        ),
        name="grad_head_chunk",
    )(*after, hidden, *grads, *extra)


def swap(x, axis, k):
    n = lax.axis_size(axis)
    return lax.ppermute(x, axis, [(i, i ^ k) for i in range(n)])


def merge_over(totals, axis, waves, mask=None):
    n = lax.axis_size(axis)
    width = totals.shape[1] // waves
    step = 1
    while step < n:
        span = min(2, n // step)
        values = [totals] + [swap(totals, axis, k * step) for k in range(1, span)]
        shifts = tuple(k * step % waves if axis == "dp" else 0 for k in range(span))
        step *= span
        totals = merge_call(values, shifts, width, mask if step == n else None)
    return totals


def rows_at(x, index, size):
    return lax.dynamic_slice_in_dim(x, index * size, size)


class Reduction:
    def __init__(self, partial, shard, own):
        self.partial, self.shard, self.own = partial, shard, own
        self.owners = lax.axis_size("mp")
        self.waves = lax.axis_size("dp") // self.owners

    def over_inner(self, flag):
        total = self.partial[0].astype(F32)
        for w in range(1, self.waves):
            total += late(swap(self.partial[w], "dp", w), flag)
        self.total = total
        return total

    def over_outer(self, flag):
        total = rows_at(self.total, self.own, self.shard)
        for a in range(1, self.owners):
            sent = rows_at(self.total, self.own ^ a, self.shard).astype(BF16)
            total += late(swap(sent, "dp", a * self.waves), flag)
        self.total = total
        return total


    def halve_vocab(self, flag):
        if lax.axis_size("vocab") != 4:
            self.total = lax.psum(self.total, "vocab")
            return self.total
        self.bit = lax.axis_index("vocab") % 2
        half = self.shard // 2
        sent = rows_at(self.total, 1 - self.bit, half).astype(BF16)
        self.total = rows_at(self.total, self.bit, half) + late(swap(sent, "vocab", 1), flag)
        return self.total

    def cross_vocab(self, flag):
        if lax.axis_size("vocab") == 4:
            sent = self.total.astype(BF16)
            self.total = sent.astype(F32) + late(swap(sent, "vocab", 2), flag)
        return self.total

    def join_vocab(self, flag):
        if lax.axis_size("vocab") == 4:
            sent = self.total.astype(BF16)
            got, kept = late(swap(sent, "vocab", 1), flag), sent.astype(F32)
            upper = self.bit == 1
            self.total = jnp.concatenate(
                [jnp.where(upper, got, kept), jnp.where(upper, kept, got)], axis=0
            )
        return self.total


def late(x, flag):
    x = x.astype(F32)
    return x if flag is None else x + flag


def per_device(hidden, head_weight, teacher_logits, response_start):
    n_dp, n_mp = lax.axis_size("dp"), lax.axis_size("mp")
    waves = n_dp // n_mp
    shard, depth = hidden.shape
    own_rows, columns = teacher_logits.shape
    mp = lax.axis_index("mp")
    dp = lax.axis_index("dp")
    outer, inner = dp // waves, dp % waves
    own = outer ^ mp
    head_t = head_weight.T
    teacher_t = teacher_logits.T

    positions = mp * own_rows + jnp.concatenate(
        [(inner ^ w) * shard + jnp.arange(shard, dtype=jnp.int32) for w in range(waves)]
    )
    sequence = positions // LEN
    seq_ids = jnp.arange(response_start.shape[0], dtype=jnp.int32)
    starts = jnp.sum(
        jnp.where(sequence[:, None] == seq_ids[None, :], response_start[None, :], 0), axis=1
    )
    mask = (positions % LEN >= starts).astype(F32)[None, :]
    chunks = chunks_of(columns, 3)
    teachers = [
        [
            lax.dynamic_slice(teacher_t, (first, (inner ^ w) * shard), (rows, shard))
            for w in range(waves)
        ]
        for first, rows in chunks
    ]

    near = {k: swap(hidden, "dp", k) for k in range(1, n_dp) if k < waves or k % waves == 0}
    pieces = [(hidden, 0, 0)]
    for k in range(1, n_dp):
        a, w = k // waves, k % waves
        if k in near:
            pieces.append((near[k], a, w * shard))
        else:
            half = shard // 2
            pieces.append((swap(near[a * waves][:half], "dp", w), a, w * shard))
            pieces.append((swap(near[w][half:], "dp", a * waves), a, w * shard + half))

    sub = 8 if columns % 8 == 0 else 1

    def exchanged(outs):
        return [outs[0]] + [swap(outs[k], "mp", k) for k in range(1, n_mp)]

    parts = []
    states = (own.astype(jnp.int32).reshape(1), pieces)
    for first, rows in chunks:
        after = [] if first else [x for chunk in teachers for x in chunk]
        outs = student_chunk(states, head_t, first, rows, n_mp, n_dp * shard, after)
        if len(outs) > n_mp:
            ordered, states = outs[n_mp:]
        parts.append(exchanged(outs[:n_mp]))
    totals = start_totals(sub, own_rows)
    for c in range(len(chunks)):
        totals = totals_chunk(parts[c], teachers[c], totals, c == len(chunks) - 1)
    totals = merge_over(totals, "dp", waves)
    coef, kl = merge_over(totals, "vocab", waves, mask)
    token_kl = jnp.zeros((1, own_rows), F32)
    for w in range(waves):
        token_kl = lax.dynamic_update_slice_in_dim(
            token_kl, kl[:, w * shard : (w + 1) * shard], (inner ^ w) * shard, 1
        )

    all_grads = []
    for c in range(len(chunks)):
        all_grads.append(exchanged([grads_chunk(parts[c], teachers[c], coef)] * n_mp))

    width = hidden_width(depth)
    tiles = depth // width
    split = (tiles + 1) // 2
    acc = None
    for c, (first, rows) in enumerate(chunks):
        last = c == len(chunks) - 1
        outs = hidden_chunk(all_grads[c], head_t, first, waves, split, acc, last)
        acc = outs[0]
    *outs, flag = outs
    one = Reduction(outs, shard, own)
    two = Reduction(hidden_rest(all_grads, head_t, waves, split, tiles - split, flag), shard, own)

    results = [one.over_inner(None)]
    plan = [
        lambda f, g: [one.over_outer(f), two.over_inner(g)],
        lambda f, g: [one.halve_vocab(f), two.over_outer(g)],
        lambda f, g: [one.cross_vocab(f), two.halve_vocab(g)],
        lambda f, g: [one.join_vocab(f), two.cross_vocab(g)],
    ]
    widths = (split * width, depth - split * width)
    calls = [(c, 0, rows) for c, (_, rows) in enumerate(chunks)]
    if calls[-1][2] % (2 * TILE) == 0:
        c, _, rows = calls.pop()
        calls += [(c, 0, rows // 2), (c, rows // 2, rows // 2)]
    grad_head = None
    for c, skip, rows in calls:
        grad_head, *flags = head_chunk(
            ordered, all_grads[c], chunks[c][0], skip, rows, columns, grad_head, results, widths
        )
        results = plan.pop(0)(*flags)
    while plan:
        results = plan.pop(0)(*flags)
    grad_hidden = jnp.concatenate([one.total, two.join_vocab(None)], axis=1)
    return (token_kl.reshape(own_rows), grad_hidden, grad_head.T)


def solution(mesh):
    return jax.shard_map(
        per_device,
        mesh=mesh,
        in_specs=(P("dp", "mp"), P("mp", ("dp", "vocab")), P("mp", ("dp", "vocab")), P()),
        out_specs=(P("mp"), P("dp", "mp"), P("mp", ("dp", "vocab"))),
        check_vma=False,
    )
```

```python
import functools

import jax
import jax.numpy as jnp
from jax import lax
from jax.experimental import pallas as pl
from jax.experimental.pallas import tpu as pltpu
from jax.sharding import PartitionSpec as P

LEN = 256
F32 = jnp.float32
BF16 = jnp.bfloat16
MIB = 1 << 20
WEIGHT = 1 / 16
TILE = 528
ALL = 63
UNREAD = pl.BlockSpec(memory_space=pl.ANY)
COLUMNS = 256


def chunks_of(total, parts):
    if total % (16 * parts):
        parts = 1
    size = total // parts
    return [(c * size, size) for c in range(parts)]


def tile_of(rows, want):
    for size in range(min(want, rows) // 16 * 16, 0, -16):
        if rows % size == 0:
            return size
    return rows


def params(mib):
    return pltpu.CompilerParams(
        dimension_semantics=("arbitrary",), vmem_limit_bytes=mib * MIB
    )


def cost(flops, moved, exps=0):
    return pl.CostEstimate(
        flops=int(flops * WEIGHT),
        bytes_accessed=int(moved * WEIGHT),
        transcendentals=int(exps * WEIGHT),
    )


def whole(shape):
    return pl.BlockSpec(shape, lambda i: (0,) * len(shape))


def fold(op, x, sub):
    if sub == 1:
        return (jnp.max if op is jnp.maximum else jnp.sum)(x, axis=0, keepdims=True)
    x = x.reshape(x.shape[0] // sub, sub, x.shape[1])
    while x.shape[0] > 1:
        half = x.shape[0] // 2
        rest = x[2 * half :]
        x = op(x[:half], x[half : 2 * half])
        if rest.shape[0]:
            x = jnp.concatenate([x, rest], axis=0)
    return x[0]


def spread(op, x, row, sub):
    if sub == 1:
        return op(x, row)
    rows, width = x.shape
    return op(x.reshape(rows // sub, sub, width), row[None]).reshape(rows, width)


def add_totals(parts, teacher_refs, state_ref, sub):
    student = parts[0][...]
    for part in parts[1:]:
        student = student + part[...]
    target = jnp.concatenate([ref[...] for ref in teacher_refs], axis=1).astype(F32)
    old = [state_ref[sub * r : sub * (r + 1)] for r in range(5)]
    top_s = jnp.maximum(old[0], fold(jnp.maximum, student, sub))
    top_t = jnp.maximum(old[1], fold(jnp.maximum, target, sub))
    exp_s = jnp.exp(spread(jnp.subtract, student, top_s, sub))
    exp_t = jnp.exp(spread(jnp.subtract, target, top_t, sub))
    scale_s = jnp.exp(old[0] - top_s)
    scale_t = jnp.exp(old[1] - top_t)
    new = [
        top_s,
        top_t,
        old[2] * scale_s + fold(jnp.add, exp_s, sub),
        old[3] * scale_t + fold(jnp.add, exp_t, sub),
        old[4] * scale_t + fold(jnp.add, exp_t * (target - student), sub),
    ]
    for r, value in enumerate(new):
        state_ref[sub * r : sub * (r + 1)] = value


def merge_classes(state_ref, sub):
    rows = [state_ref[sub * r : sub * (r + 1)] for r in range(5)]
    top_s = jnp.max(rows[0], axis=0, keepdims=True)
    top_t = jnp.max(rows[1], axis=0, keepdims=True)
    scale_s = jnp.exp(rows[0] - top_s)
    scale_t = jnp.exp(rows[1] - top_t)
    return [
        top_s,
        top_t,
        jnp.sum(rows[2] * scale_s, axis=0, keepdims=True),
        jnp.sum(rows[3] * scale_t, axis=0, keepdims=True),
        jnp.sum(rows[4] * scale_t, axis=0, keepdims=True),
    ]


def start_totals(sub, width):
    return jnp.concatenate(
        [jnp.full((2 * sub, width), -jnp.inf, F32), jnp.zeros((3 * sub, width), F32)]
    )


def totals_body(count, waves, sub, last, *refs):
    parts, teacher_refs = refs[:count], refs[count : count + waves]
    before_ref, out_ref, state_ref = refs[count + waves :]
    step = pl.program_id(0)

    @pl.when(step == 0)
    def _():
        state_ref[...] = before_ref[...]

    add_totals(parts, teacher_refs, state_ref, sub)

    @pl.when(step == pl.num_programs(0) - 1)
    def _():
        if last:
            out_ref[...] = jnp.zeros(out_ref.shape, F32)
            for r, value in enumerate(merge_classes(state_ref, sub)):
                out_ref[r : r + 1] = value
        else:
            out_ref[...] = state_ref[...]


def row_blocks(arrays, tile, skip=0):
    return [pl.BlockSpec((tile, x.shape[1]), lambda i: (i + skip, 0)) for x in arrays]


def totals_chunk(parts, teachers, before, last):
    rows, width = parts[0].shape
    sub = before.shape[0] // 5
    tile = tile_of(rows, TILE)
    out = (8 if last else 5 * sub, width)
    return pl.pallas_call(
        functools.partial(totals_body, len(parts), len(teachers), sub, last),
        grid=(rows // tile,),
        in_specs=row_blocks([*parts, *teachers], tile) + [whole(before.shape)],
        out_specs=whole(out),
        out_shape=jax.ShapeDtypeStruct(out, F32),
        scratch_shapes=[pltpu.VMEM((5 * sub, width), F32)],
        compiler_params=params(12),
        cost_estimate=cost(
            12 * rows * width, (4 * len(parts) + 2) * rows * width, 2 * rows * width
        ),
        name="totals_chunk",
    )(*parts, *teachers, before)


def student_body(owners, places, after, *refs):
    refs = list(refs[after:])
    if places is not None:
        own_ref = refs.pop(0)
        piece_refs = [refs.pop(0) for _ in places]
        turned_ref, ordered_ref = refs.pop(), refs.pop()

        for own in range(owners):

            @pl.when((pl.program_id(0) == 0) & (own_ref[0] == own))
            def _():
                for (a, at), ref in zip(places, piece_refs):
                    start = (own ^ a) * (ordered_ref.shape[0] // owners) + at
                    ordered_ref[start : start + ref.shape[0]] = ref[...]

        @pl.when(pl.program_id(0) == 0)
        def _():
            turned_ref[...] = ordered_ref[...].T

    else:
        turned_ref = refs.pop(0)
    head_ref, *out_refs = refs
    width = out_refs[0].shape[1]
    full = jnp.dot(head_ref[...], turned_ref[...], preferred_element_type=F32)
    for k, out_ref in enumerate(out_refs):
        out_ref[...] = full[:, k * width : (k + 1) * width]


def student_chunk(states, head_t, first, rows, owners, tokens, after):
    depth = head_t.shape[1]
    width = tokens // owners
    tile = tile_of(rows, TILE)
    base = first // tile
    outs = [pl.BlockSpec((tile, width), lambda i: (i, 0))] * owners
    shapes = [jax.ShapeDtypeStruct((rows, width), F32)] * owners
    places = None
    if isinstance(states, tuple):
        places = tuple((a, at) for _, a, at in states[1])
        args = [states[0]] + [x for x, _, _ in states[1]]
        specs = [pl.BlockSpec(memory_space=pltpu.SMEM)] + [whole(x.shape) for x in args[1:]]
        outs = outs + [whole((tokens, depth)), whole((depth, tokens))]
        shapes = shapes + [
            jax.ShapeDtypeStruct((tokens, depth), BF16),
            jax.ShapeDtypeStruct((depth, tokens), BF16),
        ]
    else:
        args, specs = [states], [whole((depth, tokens))]
    return pl.pallas_call(
        functools.partial(student_body, owners, places, len(after)),
        grid=(rows // tile,),
        in_specs=[UNREAD] * len(after)
        + specs
        + [pl.BlockSpec((tile, depth), lambda i: (i + base, 0))],
        out_specs=outs,
        out_shape=shapes,
        compiler_params=params(ALL),
        cost_estimate=cost(
            2 * rows * tokens * depth, 2 * rows * depth + 2 * tokens * depth + 4 * rows * tokens
        ),
        name="student_chunk",
    )(*after, *args, head_t)


def merge(refs, shifts, width):
    rows = []
    for ref, shift in zip(refs, shifts):
        x = ref[...]
        if shift:
            cut = [x[:, at : at + width] for at in range(0, x.shape[1], width)]
            x = jnp.concatenate([cut[w ^ shift] for w in range(len(cut))], axis=1)
        rows.append(x)
    top_s = functools.reduce(jnp.maximum, [x[0:1] for x in rows])
    top_t = functools.reduce(jnp.maximum, [x[1:2] for x in rows])
    terms = []
    for x in rows:
        scale_s = jnp.exp(x[0:1] - top_s)
        scale_t = jnp.exp(x[1:2] - top_t)
        terms.append([x[2:3] * scale_s, x[3:4] * scale_t, x[4:5] * scale_t])
    while len(terms) > 1:
        terms = [
            [a + b for a, b in zip(left, right)] for left, right in zip(terms[::2], terms[1::2])
        ]
    return [top_s, top_t] + terms[0]


def merge_body(shifts, width, *refs):
    *in_refs, out_ref = refs
    out_ref[...] = jnp.zeros(out_ref.shape, F32)
    for row, value in enumerate(merge(in_refs, shifts, width)):
        out_ref[row : row + 1] = value


def finish_body(shifts, width, *refs):
    *in_refs, mask_ref, coef_ref, kl_ref = refs
    top_s, top_t, sum_s, sum_t, cross = merge(in_refs, shifts, width)
    mask = mask_ref[...]
    coef_ref[...] = jnp.zeros(coef_ref.shape, F32)
    coef_ref[0:1] = top_s
    coef_ref[1:2] = top_t
    coef_ref[2:3] = mask / sum_s
    coef_ref[3:4] = mask / sum_t
    kl_ref[...] = mask * (cross / sum_t - top_t - jnp.log(sum_t) + top_s + jnp.log(sum_s))


def merge_call(values, shifts, width, mask=None):
    shape = values[0].shape
    out = jax.ShapeDtypeStruct(shape, F32)
    small = pltpu.CompilerParams(vmem_limit_bytes=2 * MIB)
    guess = cost(1 << 20, 1 << 16)
    if mask is None:
        return pl.pallas_call(
            functools.partial(merge_body, shifts, width),
            out_shape=out,
            compiler_params=small,
            cost_estimate=guess,
            name="merge_totals",
        )(*values)
    kl = jax.ShapeDtypeStruct((1, shape[1]), F32)
    return pl.pallas_call(
        functools.partial(finish_body, shifts, width),
        out_shape=(out, kl),
        compiler_params=small,
        cost_estimate=guess,
        name="finish_totals",
    )(*values, mask)


def grads_body(count, *refs):
    parts, teacher_refs = refs[:count], refs[count:-2]
    coef_ref, out_ref = refs[-2:]
    width = out_ref.shape[1] // len(teacher_refs)
    for w, teacher_ref in enumerate(teacher_refs):
        lanes = slice(w * width, (w + 1) * width)
        coef = coef_ref[:, lanes]
        student = parts[0][:, lanes]
        for part in parts[1:]:
            student = student + part[:, lanes]
        target = teacher_ref[...].astype(F32)
        out_ref[:, lanes] = (
            jnp.exp(student - coef[0:1]) * coef[2:3] - jnp.exp(target - coef[1:2]) * coef[3:4]
        ).astype(BF16)


def grads_chunk(parts, teachers, coef):
    rows, width = parts[0].shape
    tile = tile_of(rows, 2 * TILE)
    return pl.pallas_call(
        functools.partial(grads_body, len(parts)),
        grid=(rows // tile,),
        in_specs=row_blocks([*parts, *teachers], tile) + [whole(coef.shape)],
        out_specs=pl.BlockSpec((tile, width), lambda i: (i, 0)),
        out_shape=jax.ShapeDtypeStruct((rows, width), BF16),
        compiler_params=params(14),
        cost_estimate=cost(
            8 * rows * width, (4 * len(parts) + 4) * rows * width, 2 * rows * width
        ),
        name="logit_grads_chunk",
    )(*parts, *teachers, coef)


def turn(grads_refs, turned_ref):
    for k, ref in enumerate(grads_refs):
        width = ref.shape[1]
        turned_ref[k * width : (k + 1) * width] = ref[...].T


def put_rows(total, places_ref, out_ref):
    count = places_ref.shape[0]
    shard = total.shape[0] // count
    for n in range(count):
        place = pl.ds(pl.multiple_of(places_ref[n] * shard, shard), shard)
        out_ref[place] = total[n * shard : (n + 1) * shard].astype(BF16)


def hidden_body(count, has_acc, last, *refs):
    places_ref, *refs = refs
    grads_refs, head_ref, *rest = (refs[:count], *refs[count:])
    before_ref = rest.pop(0) if has_acc else None
    out_ref, *flag_refs, turned_ref = rest

    @pl.when(pl.program_id(0) == 0)
    def _():
        turn(grads_refs, turned_ref)

    total = jnp.dot(turned_ref[...], head_ref[...], preferred_element_type=F32)
    if has_acc:
        total = total + before_ref[...]
    if last:
        flag_refs[0][...] = jnp.zeros(flag_refs[0].shape, F32)
        put_rows(total, places_ref, out_ref)
    else:
        out_ref[...] = total


def hidden_width(depth):
    return COLUMNS if depth % COLUMNS == 0 else 128


def hidden_chunk(places, grads, head_t, first, tiles, before, last):
    rows = grads[0].shape[0]
    width = hidden_width(head_t.shape[1])
    base = first // rows
    tokens = sum(g.shape[1] for g in grads)
    size = tiles * width
    block = pl.BlockSpec((tokens, width), lambda i: (0, i))
    has_acc = before is not None
    flag = jax.ShapeDtypeStruct((8, 128), F32)
    return pl.pallas_call(
        functools.partial(hidden_body, len(grads), has_acc, last),
        grid=(tiles,),
        in_specs=[pl.BlockSpec(memory_space=pltpu.SMEM)]
        + [whole(g.shape) for g in grads]
        + [pl.BlockSpec((rows, width), lambda i: (base, i))]
        + [block] * has_acc,
        out_specs=[block] + [whole(flag.shape)] * last,
        out_shape=[jax.ShapeDtypeStruct((tokens, size), BF16 if last else F32)] + [flag] * last,
        scratch_shapes=[pltpu.VMEM((tokens, rows), BF16)],
        compiler_params=params(30),
        cost_estimate=cost(2 * rows * tokens * size, 2 * rows * (size + tokens)),
        name="grad_hidden_chunk",
    )(places, *grads, head_t, *([before] if has_acc else []))


def hidden_rest_body(chunks, owners, *refs):
    places_ref, *refs = refs[1:]
    grads_refs = refs[: chunks * owners]
    head_ref, out_ref, turned_ref, acc_ref = refs[chunks * owners :]
    tile, chunk = pl.program_id(0), pl.program_id(1)
    for c in range(chunks):

        @pl.when((tile == 0) & (chunk == c))
        def _():
            turn(grads_refs[c * owners : (c + 1) * owners], turned_ref.at[c])

    term = jnp.dot(turned_ref[chunk], head_ref[...], preferred_element_type=F32)

    @pl.when(chunk == 0)
    def _():
        acc_ref[...] = term

    @pl.when(chunk > 0)
    def _():
        acc_ref[...] += term

    @pl.when(chunk == chunks - 1)
    def _():
        put_rows(acc_ref[...], places_ref, out_ref)


def hidden_rest(places, all_grads, head_t, tile, tiles, flag):
    chunks, owners = len(all_grads), len(all_grads[0])
    grads = [g for chunk in all_grads for g in chunk]
    rows, per_owner = grads[0].shape
    tokens = owners * per_owner
    width = hidden_width(head_t.shape[1])
    size = tiles * width
    full = lambda shape: pl.BlockSpec(shape, lambda i, c: (0, 0))
    return pl.pallas_call(
        functools.partial(hidden_rest_body, chunks, owners),
        grid=(tiles, chunks),
        in_specs=[UNREAD, pl.BlockSpec(memory_space=pltpu.SMEM)]
        + [full(g.shape) for g in grads]
        + [pl.BlockSpec((rows, width), lambda i, c: (c, i + tile))],
        out_specs=pl.BlockSpec((tokens, width), lambda i, c: (0, i)),
        out_shape=jax.ShapeDtypeStruct((tokens, size), BF16),
        scratch_shapes=[
            pltpu.VMEM((chunks, tokens, rows), BF16),
            pltpu.VMEM((tokens, width), F32),
        ],
        compiler_params=pltpu.CompilerParams(
            dimension_semantics=("arbitrary", "arbitrary"), vmem_limit_bytes=38 * MIB
        ),
        cost_estimate=cost(
            2 * chunks * rows * tokens * size, 2 * chunks * rows * (size + tokens)
        ),
        name="grad_hidden_rest",
    )(flag, places, *grads, head_t)


def head_body(count, after, *refs):
    hidden_ref, *refs = refs[after:]
    grads = jnp.concatenate([ref[...] for ref in refs[:count]], axis=1)
    out_ref, flag_ref = refs[-2:]

    @pl.when(pl.program_id(0) == 0)
    def _():
        flag_ref[...] = jnp.zeros(flag_ref.shape, F32)

    for at in range(0, out_ref.shape[1], COLUMNS):
        lanes = slice(at, min(at + COLUMNS, out_ref.shape[1]))
        out_ref[:, lanes] = jnp.dot(
            grads, hidden_ref[:, lanes], preferred_element_type=F32
        ).astype(BF16)


def head_chunk(hidden, grads, first, skip, rows, total, before, after):
    tokens, depth = hidden.shape
    tile = tile_of(rows, TILE)
    base = (first + skip) // tile
    specs = [UNREAD] * len(after) + [whole(hidden.shape)] + row_blocks(grads, tile, skip // tile)
    extra, aliases = [], {}
    if before is not None:
        specs.append(UNREAD)
        extra, aliases = [before], {len(after) + 1 + len(grads): 0}
    return pl.pallas_call(
        functools.partial(head_body, len(grads), len(after)),
        grid=(rows // tile,),
        in_specs=specs,
        out_specs=[pl.BlockSpec((tile, depth), lambda i: (i + base, 0)), whole((1, depth))],
        out_shape=[
            jax.ShapeDtypeStruct((total, depth), BF16),
            jax.ShapeDtypeStruct((1, depth), F32),
        ],
        input_output_aliases=aliases,
        compiler_params=params(24),
        cost_estimate=cost(
            2 * rows * tokens * depth, 2 * rows * depth + 2 * tokens * depth + 2 * rows * tokens
        ),
        name="grad_head_chunk",
    )(*after, hidden, *grads, *extra)


def swap(x, axis, k):
    n = lax.axis_size(axis)
    return lax.ppermute(x, axis, [(i, i ^ k) for i in range(n)])


def merge_over(totals, axis, waves, mask=None):
    n = lax.axis_size(axis)
    width = totals.shape[1] // waves
    step = 1
    while step < n:
        span = min(2, n // step)
        values = [totals] + [swap(totals, axis, k * step) for k in range(1, span)]
        shifts = tuple(k * step % waves if axis == "dp" else 0 for k in range(span))
        step *= span
        totals = merge_call(values, shifts, width, mask if step == n else None)
    return totals


def once_there(x, *others):
    return pl.pallas_call(
        lambda *refs: None,
        in_specs=[UNREAD] * (1 + len(others)),
        out_specs=UNREAD,
        out_shape=jax.ShapeDtypeStruct(x.shape, x.dtype),
        input_output_aliases={0: 0},
        compiler_params=pltpu.CompilerParams(vmem_limit_bytes=MIB),
        cost_estimate=cost(0, 0),
        name="once_there",
    )(x, *others)


def per_device(hidden, head_weight, teacher_logits, response_start):
    n_dp, n_mp = lax.axis_size("dp"), lax.axis_size("mp")
    waves = n_dp // n_mp
    shard, depth = hidden.shape
    own_rows, columns = teacher_logits.shape
    mp = lax.axis_index("mp")
    dp = lax.axis_index("dp")
    outer, inner = dp // waves, dp % waves
    own = outer ^ mp
    head_t = head_weight.T
    teacher_t = teacher_logits.T

    positions = mp * own_rows + jnp.concatenate(
        [(inner ^ w) * shard + jnp.arange(shard, dtype=jnp.int32) for w in range(waves)]
    )
    sequence = positions // LEN
    seq_ids = jnp.arange(response_start.shape[0], dtype=jnp.int32)
    starts = jnp.sum(
        jnp.where(sequence[:, None] == seq_ids[None, :], response_start[None, :], 0), axis=1
    )
    mask = (positions % LEN >= starts).astype(F32)[None, :]
    chunks = chunks_of(columns, 3)
    teachers = [
        [
            lax.dynamic_slice(teacher_t, (first, (inner ^ w) * shard), (rows, shard))
            for w in range(waves)
        ]
        for first, rows in chunks
    ]

    near = {k: swap(hidden, "dp", k) for k in range(1, n_dp) if k < waves or k % waves == 0}
    pieces = [(hidden, 0, 0)]
    for k in range(1, n_dp):
        a, w = k // waves, k % waves
        if k in near:
            pieces.append((near[k], a, w * shard))
        else:
            half = shard // 2
            pieces.append((swap(near[a * waves][:half], "dp", w), a, w * shard))
            pieces.append((swap(near[w][half:], "dp", a * waves), a, w * shard + half))

    sub = 8 if columns % 8 == 0 else 1

    def exchanged(outs):
        return [outs[0]] + [swap(outs[k], "mp", k) for k in range(1, n_mp)]

    parts = []
    states = (own.astype(jnp.int32).reshape(1), pieces)
    for first, rows in chunks:
        after = [] if first else [x for chunk in teachers for x in chunk]
        outs = student_chunk(states, head_t, first, rows, n_mp, n_dp * shard, after)
        if len(outs) > n_mp:
            ordered, states = outs[n_mp:]
        parts.append(exchanged(outs[:n_mp]))
    totals = start_totals(sub, own_rows)
    for c in range(len(chunks)):
        totals = totals_chunk(parts[c], teachers[c], totals, c == len(chunks) - 1)
    totals = merge_over(totals, "dp", waves)
    coef, kl = merge_over(totals, "vocab", waves, mask)
    token_kl = jnp.zeros((1, own_rows), F32)
    for w in range(waves):
        token_kl = lax.dynamic_update_slice_in_dim(
            token_kl, kl[:, w * shard : (w + 1) * shard], (inner ^ w) * shard, 1
        )

    all_grads = []
    for c in range(len(chunks)):
        all_grads.append(exchanged([grads_chunk(parts[c], teachers[c], coef)] * n_mp))

    width = hidden_width(depth)
    tiles = depth // width
    split = (tiles + 1) // 2
    places = jnp.stack(
        [(mp ^ k) * waves + (inner ^ w) for k in range(n_mp) for w in range(waves)]
    ).astype(jnp.int32)
    acc = None
    for c, (first, rows) in enumerate(chunks):
        last = c == len(chunks) - 1
        acc, *flags = hidden_chunk(places, all_grads[c], head_t, first, split, acc, last)
    scattered = lax.psum_scatter(acc, "dp", scatter_dimension=0, tiled=True)
    rest = hidden_rest(places, all_grads, head_t, split, tiles - split, flags[0])
    two = lax.psum_scatter(rest, "dp", scatter_dimension=0, tiled=True)
    one = lax.psum(scattered, "vocab")

    grad_head, flag = None, scattered
    for c, (first, rows) in enumerate(chunks):
        if c == len(chunks) - 1:
            two = once_there(two, one, flag)
        after = [scattered] if c == 0 else [two] if c == len(chunks) - 1 else []
        grad_head, flag = head_chunk(
            ordered, all_grads[c], first, 0, rows, columns, grad_head, after
        )
    two = lax.psum(two, "vocab")
    grad_hidden = jnp.concatenate([one, two], axis=1).astype(F32) + flag
    return (token_kl.reshape(own_rows), grad_hidden, grad_head.T)


def solution(mesh):
    return jax.shard_map(
        per_device,
        mesh=mesh,
        in_specs=(P("dp", "mp"), P("mp", ("dp", "vocab")), P("mp", ("dp", "vocab")), P()),
        out_specs=(P("mp"), P("dp", "mp"), P("mp", ("dp", "vocab"))),
        check_vma=False,
    )
```

```python
import functools

import jax
import jax.numpy as jnp
from jax import lax
from jax.experimental import pallas as pl
from jax.experimental.pallas import tpu as pltpu
from jax.sharding import PartitionSpec as P

LEN = 256
F32 = jnp.float32
BF16 = jnp.bfloat16
MIB = 1 << 20
WEIGHT = 1 / 16
TILE = 528
ALL = 63
UNREAD = pl.BlockSpec(memory_space=pl.ANY)
COLUMNS = 256


def chunks_of(total, parts):
    if total % (16 * parts):
        parts = 1
    size = total // parts
    return [(c * size, size) for c in range(parts)]


def tile_of(rows, want):
    for size in range(min(want, rows) // 16 * 16, 0, -16):
        if rows % size == 0:
            return size
    return rows


def params(mib):
    return pltpu.CompilerParams(
        dimension_semantics=("arbitrary",), vmem_limit_bytes=mib * MIB
    )


def cost(flops, moved, exps=0):
    return pl.CostEstimate(
        flops=int(flops * WEIGHT),
        bytes_accessed=int(moved * WEIGHT),
        transcendentals=int(exps * WEIGHT),
    )


def whole(shape):
    return pl.BlockSpec(shape, lambda i: (0,) * len(shape))


def fold(op, x, sub):
    if sub == 1:
        return (jnp.max if op is jnp.maximum else jnp.sum)(x, axis=0, keepdims=True)
    x = x.reshape(x.shape[0] // sub, sub, x.shape[1])
    while x.shape[0] > 1:
        half = x.shape[0] // 2
        rest = x[2 * half :]
        x = op(x[:half], x[half : 2 * half])
        if rest.shape[0]:
            x = jnp.concatenate([x, rest], axis=0)
    return x[0]


def spread(op, x, row, sub):
    if sub == 1:
        return op(x, row)
    rows, width = x.shape
    return op(x.reshape(rows // sub, sub, width), row[None]).reshape(rows, width)


def add_totals(parts, teacher_refs, state_ref, sub):
    student = parts[0][...]
    for part in parts[1:]:
        student = student + part[...]
    target = jnp.concatenate([ref[...] for ref in teacher_refs], axis=1).astype(F32)
    old = [state_ref[sub * r : sub * (r + 1)] for r in range(5)]
    top_s = jnp.maximum(old[0], fold(jnp.maximum, student, sub))
    top_t = jnp.maximum(old[1], fold(jnp.maximum, target, sub))
    exp_s = jnp.exp(spread(jnp.subtract, student, top_s, sub))
    exp_t = jnp.exp(spread(jnp.subtract, target, top_t, sub))
    scale_s = jnp.exp(old[0] - top_s)
    scale_t = jnp.exp(old[1] - top_t)
    new = [
        top_s,
        top_t,
        old[2] * scale_s + fold(jnp.add, exp_s, sub),
        old[3] * scale_t + fold(jnp.add, exp_t, sub),
        old[4] * scale_t + fold(jnp.add, exp_t * (target - student), sub),
    ]
    for r, value in enumerate(new):
        state_ref[sub * r : sub * (r + 1)] = value


def merge_classes(state_ref, sub):
    rows = [state_ref[sub * r : sub * (r + 1)] for r in range(5)]
    top_s = jnp.max(rows[0], axis=0, keepdims=True)
    top_t = jnp.max(rows[1], axis=0, keepdims=True)
    scale_s = jnp.exp(rows[0] - top_s)
    scale_t = jnp.exp(rows[1] - top_t)
    return [
        top_s,
        top_t,
        jnp.sum(rows[2] * scale_s, axis=0, keepdims=True),
        jnp.sum(rows[3] * scale_t, axis=0, keepdims=True),
        jnp.sum(rows[4] * scale_t, axis=0, keepdims=True),
    ]


def start_totals(sub, width):
    return jnp.concatenate(
        [jnp.full((2 * sub, width), -jnp.inf, F32), jnp.zeros((3 * sub, width), F32)]
    )


def totals_body(count, waves, sub, last, *refs):
    parts, teacher_refs = refs[:count], refs[count : count + waves]
    before_ref, out_ref, state_ref = refs[count + waves :]
    step = pl.program_id(0)

    @pl.when(step == 0)
    def _():
        state_ref[...] = before_ref[...]

    add_totals(parts, teacher_refs, state_ref, sub)

    @pl.when(step == pl.num_programs(0) - 1)
    def _():
        if last:
            out_ref[...] = jnp.zeros(out_ref.shape, F32)
            for r, value in enumerate(merge_classes(state_ref, sub)):
                out_ref[r : r + 1] = value
        else:
            out_ref[...] = state_ref[...]


def row_blocks(arrays, tile):
    return [pl.BlockSpec((tile, x.shape[1]), lambda i: (i, 0)) for x in arrays]


def totals_chunk(parts, teachers, before, last):
    rows, width = parts[0].shape
    sub = before.shape[0] // 5
    tile = tile_of(rows, TILE)
    out = (8 if last else 5 * sub, width)
    return pl.pallas_call(
        functools.partial(totals_body, len(parts), len(teachers), sub, last),
        grid=(rows // tile,),
        in_specs=row_blocks([*parts, *teachers], tile) + [whole(before.shape)],
        out_specs=whole(out),
        out_shape=jax.ShapeDtypeStruct(out, F32),
        scratch_shapes=[pltpu.VMEM((5 * sub, width), F32)],
        compiler_params=params(12),
        cost_estimate=cost(
            12 * rows * width, (4 * len(parts) + 2) * rows * width, 2 * rows * width
        ),
        name="totals_chunk",
    )(*parts, *teachers, before)


def student_body(owners, places, after, *refs):
    refs = list(refs[after:])
    if places is not None:
        own_ref = refs.pop(0)
        piece_refs = [refs.pop(0) for _ in places]
        turned_ref, ordered_ref = refs.pop(), refs.pop()

        for own in range(owners):

            @pl.when((pl.program_id(0) == 0) & (own_ref[0] == own))
            def _():
                for (a, at), ref in zip(places, piece_refs):
                    start = (own ^ a) * (ordered_ref.shape[0] // owners) + at
                    ordered_ref[start : start + ref.shape[0]] = ref[...]

        @pl.when(pl.program_id(0) == 0)
        def _():
            turned_ref[...] = ordered_ref[...].T

    else:
        turned_ref = refs.pop(0)
    head_ref, *out_refs = refs
    width = out_refs[0].shape[1]
    full = jnp.dot(head_ref[...], turned_ref[...], preferred_element_type=F32)
    for k, out_ref in enumerate(out_refs):
        out_ref[...] = full[:, k * width : (k + 1) * width]


def student_chunk(states, head_t, first, rows, owners, tokens, after):
    depth = head_t.shape[1]
    width = tokens // owners
    tile = tile_of(rows, TILE)
    base = first // tile
    outs = [pl.BlockSpec((tile, width), lambda i: (i, 0))] * owners
    shapes = [jax.ShapeDtypeStruct((rows, width), F32)] * owners
    places = None
    if isinstance(states, tuple):
        places = tuple((a, at) for _, a, at in states[1])
        args = [states[0]] + [x for x, _, _ in states[1]]
        specs = [pl.BlockSpec(memory_space=pltpu.SMEM)] + [whole(x.shape) for x in args[1:]]
        outs = outs + [whole((tokens, depth)), whole((depth, tokens))]
        shapes = shapes + [
            jax.ShapeDtypeStruct((tokens, depth), BF16),
            jax.ShapeDtypeStruct((depth, tokens), BF16),
        ]
    else:
        args, specs = [states], [whole((depth, tokens))]
    return pl.pallas_call(
        functools.partial(student_body, owners, places, len(after)),
        grid=(rows // tile,),
        in_specs=[UNREAD] * len(after)
        + specs
        + [pl.BlockSpec((tile, depth), lambda i: (i + base, 0))],
        out_specs=outs,
        out_shape=shapes,
        compiler_params=params(ALL),
        cost_estimate=cost(
            2 * rows * tokens * depth, 2 * rows * depth + 2 * tokens * depth + 4 * rows * tokens
        ),
        name="student_chunk",
    )(*after, *args, head_t)


def merge(refs, shifts, width):
    rows = []
    for ref, shift in zip(refs, shifts):
        x = ref[...]
        if shift:
            cut = [x[:, at : at + width] for at in range(0, x.shape[1], width)]
            x = jnp.concatenate([cut[w ^ shift] for w in range(len(cut))], axis=1)
        rows.append(x)
    top_s = functools.reduce(jnp.maximum, [x[0:1] for x in rows])
    top_t = functools.reduce(jnp.maximum, [x[1:2] for x in rows])
    terms = []
    for x in rows:
        scale_s = jnp.exp(x[0:1] - top_s)
        scale_t = jnp.exp(x[1:2] - top_t)
        terms.append([x[2:3] * scale_s, x[3:4] * scale_t, x[4:5] * scale_t])
    while len(terms) > 1:
        terms = [
            [a + b for a, b in zip(left, right)] for left, right in zip(terms[::2], terms[1::2])
        ]
    return [top_s, top_t] + terms[0]


def merge_body(shifts, width, *refs):
    *in_refs, out_ref = refs
    out_ref[...] = jnp.zeros(out_ref.shape, F32)
    for row, value in enumerate(merge(in_refs, shifts, width)):
        out_ref[row : row + 1] = value


def finish_body(shifts, width, *refs):
    *in_refs, mask_ref, coef_ref, kl_ref = refs
    top_s, top_t, sum_s, sum_t, cross = merge(in_refs, shifts, width)
    mask = mask_ref[...]
    coef_ref[...] = jnp.zeros(coef_ref.shape, F32)
    coef_ref[0:1] = top_s
    coef_ref[1:2] = top_t
    coef_ref[2:3] = mask / sum_s
    coef_ref[3:4] = mask / sum_t
    kl_ref[...] = mask * (cross / sum_t - top_t - jnp.log(sum_t) + top_s + jnp.log(sum_s))


def merge_call(values, shifts, width, mask=None):
    shape = values[0].shape
    out = jax.ShapeDtypeStruct(shape, F32)
    small = pltpu.CompilerParams(vmem_limit_bytes=2 * MIB)
    guess = cost(1 << 20, 1 << 16)
    if mask is None:
        return pl.pallas_call(
            functools.partial(merge_body, shifts, width),
            out_shape=out,
            compiler_params=small,
            cost_estimate=guess,
            name="merge_totals",
        )(*values)
    kl = jax.ShapeDtypeStruct((1, shape[1]), F32)
    return pl.pallas_call(
        functools.partial(finish_body, shifts, width),
        out_shape=(out, kl),
        compiler_params=small,
        cost_estimate=guess,
        name="finish_totals",
    )(*values, mask)


def grads_body(count, *refs):
    parts, teacher_refs = refs[:count], refs[count:-2]
    coef_ref, out_ref = refs[-2:]
    width = out_ref.shape[1] // len(teacher_refs)
    for w, teacher_ref in enumerate(teacher_refs):
        lanes = slice(w * width, (w + 1) * width)
        coef = coef_ref[:, lanes]
        student = parts[0][:, lanes]
        for part in parts[1:]:
            student = student + part[:, lanes]
        target = teacher_ref[...].astype(F32)
        out_ref[:, lanes] = (
            jnp.exp(student - coef[0:1]) * coef[2:3] - jnp.exp(target - coef[1:2]) * coef[3:4]
        ).astype(BF16)


def grads_chunk(parts, teachers, coef):
    rows, width = parts[0].shape
    tile = tile_of(rows, 2 * TILE)
    return pl.pallas_call(
        functools.partial(grads_body, len(parts)),
        grid=(rows // tile,),
        in_specs=row_blocks([*parts, *teachers], tile) + [whole(coef.shape)],
        out_specs=pl.BlockSpec((tile, width), lambda i: (i, 0)),
        out_shape=jax.ShapeDtypeStruct((rows, width), BF16),
        compiler_params=params(14),
        cost_estimate=cost(
            8 * rows * width, (4 * len(parts) + 4) * rows * width, 2 * rows * width
        ),
        name="logit_grads_chunk",
    )(*parts, *teachers, coef)


def turn(grads_refs, turned_ref):
    for k, ref in enumerate(grads_refs):
        width = ref.shape[1]
        turned_ref[k * width : (k + 1) * width] = ref[...].T


def put_waves(total, owners, out_refs):
    waves = len(out_refs)
    shard = total.shape[0] // (owners * waves)
    for k in range(owners):
        for w, out_ref in enumerate(out_refs):
            at = (k * waves + w) * shard
            out_ref[k * shard : (k + 1) * shard] = total[at : at + shard].astype(BF16)


def hidden_body(count, has_acc, last, *refs):
    grads_refs, head_ref, *rest = (refs[:count], *refs[count:])
    before_ref = rest.pop(0) if has_acc else None
    *out_refs, turned_ref = rest

    @pl.when(pl.program_id(0) == 0)
    def _():
        turn(grads_refs, turned_ref)

    total = jnp.dot(turned_ref[...], head_ref[...], preferred_element_type=F32)
    if has_acc:
        total = total + before_ref[...]
    if last:
        *out_refs, flag_ref = out_refs
        flag_ref[...] = jnp.zeros(flag_ref.shape, F32)
        put_waves(total, count, out_refs)
    else:
        out_refs[0][...] = total


def hidden_width(depth):
    return COLUMNS if depth % COLUMNS == 0 else 128


def hidden_chunk(grads, head_t, first, waves, tiles, before, last):
    rows = grads[0].shape[0]
    width = hidden_width(head_t.shape[1])
    base = first // rows
    tokens = sum(g.shape[1] for g in grads)
    size = tiles * width
    pieces = waves if last else 1
    block = lambda count: pl.BlockSpec((count, width), lambda i: (0, i))
    has_acc = before is not None
    flag = jax.ShapeDtypeStruct((8, 128), F32)
    return pl.pallas_call(
        functools.partial(hidden_body, len(grads), has_acc, last),
        grid=(tiles,),
        in_specs=[whole(g.shape) for g in grads]
        + [pl.BlockSpec((rows, width), lambda i: (base, i))]
        + [block(tokens)] * has_acc,
        out_specs=[block(tokens // pieces)] * pieces + [whole(flag.shape)] * last,
        out_shape=[jax.ShapeDtypeStruct((tokens // pieces, size), BF16 if last else F32)] * pieces
        + [flag] * last,
        scratch_shapes=[pltpu.VMEM((tokens, rows), BF16)],
        compiler_params=params(30),
        cost_estimate=cost(2 * rows * tokens * size, 2 * rows * (size + tokens)),
        name="grad_hidden_chunk",
    )(*grads, head_t, *([before] if has_acc else []))


def hidden_rest_body(chunks, owners, *refs):
    grads_refs, head_ref, *out_refs = refs[1 : 1 + chunks * owners], *refs[1 + chunks * owners :]
    *out_refs, turned_ref, acc_ref = out_refs
    tile, chunk = pl.program_id(0), pl.program_id(1)
    for c in range(chunks):

        @pl.when((tile == 0) & (chunk == c))
        def _():
            turn(grads_refs[c * owners : (c + 1) * owners], turned_ref.at[c])

    term = jnp.dot(turned_ref[chunk], head_ref[...], preferred_element_type=F32)

    @pl.when(chunk == 0)
    def _():
        acc_ref[...] = term

    @pl.when(chunk > 0)
    def _():
        acc_ref[...] += term

    @pl.when(chunk == chunks - 1)
    def _():
        put_waves(acc_ref[...], owners, out_refs)


def hidden_rest(all_grads, head_t, waves, tile, tiles, flag):
    chunks, owners = len(all_grads), len(all_grads[0])
    grads = [g for chunk in all_grads for g in chunk]
    rows, per_owner = grads[0].shape
    tokens = owners * per_owner
    width = hidden_width(head_t.shape[1])
    size = tiles * width
    full = lambda shape: pl.BlockSpec(shape, lambda i, c: (0, 0))
    return pl.pallas_call(
        functools.partial(hidden_rest_body, chunks, owners),
        grid=(tiles, chunks),
        in_specs=[UNREAD]
        + [full(g.shape) for g in grads]
        + [pl.BlockSpec((rows, width), lambda i, c: (c, i + tile))],
        out_specs=[pl.BlockSpec((tokens // waves, width), lambda i, c: (0, i))] * waves,
        out_shape=[jax.ShapeDtypeStruct((tokens // waves, size), BF16)] * waves,
        scratch_shapes=[
            pltpu.VMEM((chunks, tokens, rows), BF16),
            pltpu.VMEM((tokens, width), F32),
        ],
        compiler_params=pltpu.CompilerParams(
            dimension_semantics=("arbitrary", "arbitrary"), vmem_limit_bytes=58 * MIB
        ),
        cost_estimate=cost(
            2 * chunks * rows * tokens * size, 2 * chunks * rows * (size + tokens)
        ),
        name="grad_hidden_rest",
    )(flag, *grads, head_t)


def head_body(count, after, *refs):
    hidden_ref, *refs = refs[after:]
    grads = jnp.concatenate([ref[...] for ref in refs[:count]], axis=1)
    out_ref, *flag_refs = refs[-3:]

    @pl.when(pl.program_id(0) == 0)
    def _():
        for ref in flag_refs:
            ref[...] = jnp.zeros(ref.shape, F32)

    for at in range(0, out_ref.shape[1], COLUMNS):
        lanes = slice(at, min(at + COLUMNS, out_ref.shape[1]))
        out_ref[:, lanes] = jnp.dot(
            grads, hidden_ref[:, lanes], preferred_element_type=F32
        ).astype(BF16)


def head_chunk(hidden, grads, first, rows, total, before, after, widths):
    tokens, depth = hidden.shape
    tile = tile_of(rows, TILE)
    base = first // tile
    specs = [UNREAD] * len(after) + [whole(hidden.shape)] + row_blocks(grads, tile)
    extra, aliases = [], {}
    if before is not None:
        specs.append(UNREAD)
        extra, aliases = [before], {len(after) + 1 + len(grads): 0}
    return pl.pallas_call(
        functools.partial(head_body, len(grads), len(after)),
        grid=(rows // tile,),
        in_specs=specs,
        out_specs=[pl.BlockSpec((tile, depth), lambda i: (i + base, 0))]
        + [whole((1, n)) for n in widths],
        out_shape=[jax.ShapeDtypeStruct((total, depth), BF16)]
        + [jax.ShapeDtypeStruct((1, n), F32) for n in widths],
        input_output_aliases=aliases,
        compiler_params=params(24),
        cost_estimate=cost(
            2 * rows * tokens * depth, 2 * rows * depth + 2 * tokens * depth + 2 * rows * tokens
        ),
        name="grad_head_chunk",
    )(*after, hidden, *grads, *extra)


def swap(x, axis, k):
    n = lax.axis_size(axis)
    return lax.ppermute(x, axis, [(i, i ^ k) for i in range(n)])


def merge_over(totals, axis, waves, mask=None):
    n = lax.axis_size(axis)
    width = totals.shape[1] // waves
    step = 1
    while step < n:
        span = min(2, n // step)
        values = [totals] + [swap(totals, axis, k * step) for k in range(1, span)]
        shifts = tuple(k * step % waves if axis == "dp" else 0 for k in range(span))
        step *= span
        totals = merge_call(values, shifts, width, mask if step == n else None)
    return totals


def rows_at(x, index, size):
    return lax.dynamic_slice_in_dim(x, index * size, size)


class Reduction:
    def __init__(self, partial, shard, own):
        self.partial, self.shard, self.own = partial, shard, own
        self.owners = lax.axis_size("mp")
        self.waves = lax.axis_size("dp") // self.owners

    def over_inner(self, flag):
        total = self.partial[0].astype(F32)
        for w in range(1, self.waves):
            total += late(swap(self.partial[w], "dp", w), flag)
        self.total = total
        return total

    def over_outer(self, flag):
        total = rows_at(self.total, self.own, self.shard)
        for a in range(1, self.owners):
            sent = rows_at(self.total, self.own ^ a, self.shard).astype(BF16)
            total += late(swap(sent, "dp", a * self.waves), flag)
        self.total = total
        return total


    def scatter_vocab(self, flag):
        n = lax.axis_size("vocab")
        if n > 4 or self.shard % (8 * n):
            self.block = lax.psum(self.total, "vocab")
            return self.block
        mine, size = lax.axis_index("vocab"), self.shard // n
        block = rows_at(self.total, mine, size)
        for c in range(1, n):
            sent = rows_at(self.total, mine ^ c, size).astype(BF16)
            block += late(swap(sent, "vocab", c), flag)
        self.block = block.astype(BF16)
        return self.block


def gather_vocab(blocks, shard):
    block = jnp.concatenate(blocks, axis=1)
    size = block.shape[0]
    if size == shard:
        return block
    mine = lax.axis_index("vocab")
    result = jnp.zeros((shard, block.shape[1]), F32)
    for c in range(lax.axis_size("vocab")):
        piece = swap(block, "vocab", c) if c else block
        result = lax.dynamic_update_slice_in_dim(
            result, piece.astype(F32), (mine ^ c) * size, 0
        )
    return result


def late(x, flag):
    x = x.astype(F32)
    return x if flag is None else x + flag


def per_device(hidden, head_weight, teacher_logits, response_start):
    n_dp, n_mp = lax.axis_size("dp"), lax.axis_size("mp")
    waves = n_dp // n_mp
    shard, depth = hidden.shape
    own_rows, columns = teacher_logits.shape
    mp = lax.axis_index("mp")
    dp = lax.axis_index("dp")
    outer, inner = dp // waves, dp % waves
    own = outer ^ mp
    head_t = head_weight.T
    teacher_t = teacher_logits.T

    positions = mp * own_rows + jnp.concatenate(
        [(inner ^ w) * shard + jnp.arange(shard, dtype=jnp.int32) for w in range(waves)]
    )
    sequence = positions // LEN
    seq_ids = jnp.arange(response_start.shape[0], dtype=jnp.int32)
    starts = jnp.sum(
        jnp.where(sequence[:, None] == seq_ids[None, :], response_start[None, :], 0), axis=1
    )
    mask = (positions % LEN >= starts).astype(F32)[None, :]
    chunks = chunks_of(columns, 3)
    teachers = [
        [
            lax.dynamic_slice(teacher_t, (first, (inner ^ w) * shard), (rows, shard))
            for w in range(waves)
        ]
        for first, rows in chunks
    ]

    near = {k: swap(hidden, "dp", k) for k in range(1, n_dp) if k < waves or k % waves == 0}
    pieces = [(hidden, 0, 0)]
    for k in range(1, n_dp):
        a, w = k // waves, k % waves
        if k in near:
            pieces.append((near[k], a, w * shard))
        else:
            half = shard // 2
            pieces.append((swap(near[a * waves][:half], "dp", w), a, w * shard))
            pieces.append((swap(near[w][half:], "dp", a * waves), a, w * shard + half))

    sub = 8 if columns % 8 == 0 else 1

    def exchanged(outs):
        return [outs[0]] + [swap(outs[k], "mp", k) for k in range(1, n_mp)]

    parts = []
    states = (own.astype(jnp.int32).reshape(1), pieces)
    for first, rows in chunks:
        after = [] if first else [x for chunk in teachers for x in chunk]
        outs = student_chunk(states, head_t, first, rows, n_mp, n_dp * shard, after)
        if len(outs) > n_mp:
            ordered, states = outs[n_mp:]
        parts.append(exchanged(outs[:n_mp]))
    totals = start_totals(sub, own_rows)
    for c in range(len(chunks)):
        totals = totals_chunk(parts[c], teachers[c], totals, c == len(chunks) - 1)
    totals = merge_over(totals, "dp", waves)
    coef, kl = merge_over(totals, "vocab", waves, mask)
    token_kl = jnp.zeros((1, own_rows), F32)
    for w in range(waves):
        token_kl = lax.dynamic_update_slice_in_dim(
            token_kl, kl[:, w * shard : (w + 1) * shard], (inner ^ w) * shard, 1
        )

    all_grads = []
    for c in range(len(chunks)):
        all_grads.append(exchanged([grads_chunk(parts[c], teachers[c], coef)] * n_mp))

    width = hidden_width(depth)
    tiles = depth // width
    split = (tiles + 1) // 2
    acc = None
    for c, (first, rows) in enumerate(chunks):
        last = c == len(chunks) - 1
        outs = hidden_chunk(all_grads[c], head_t, first, waves, split, acc, last)
        acc = outs[0]
    *outs, flag = outs
    one = Reduction(outs, shard, own)
    two = Reduction(hidden_rest(all_grads, head_t, waves, split, tiles - split, flag), shard, own)

    results = [one.over_inner(None)]
    plan = [
        lambda f, g: [one.over_outer(f), two.over_inner(g)],
        lambda f, g: [one.scatter_vocab(f), two.over_outer(g)],
        lambda f, g: [one.block, two.scatter_vocab(g)],
    ]
    widths = (split * width, depth - split * width)
    grad_head = None
    for c, (first, rows) in enumerate(chunks):
        grad_head, *flags = head_chunk(
            ordered, all_grads[c], first, rows, columns, grad_head, results, widths
        )
        results = plan.pop(0)(*flags)
    while plan:
        results = plan.pop(0)(*flags)
    grad_hidden = gather_vocab([one.block, two.block], shard)
    return (token_kl.reshape(own_rows), grad_hidden, grad_head.T)


def solution(mesh):
    return jax.shard_map(
        per_device,
        mesh=mesh,
        in_specs=(P("dp", "mp"), P("mp", ("dp", "vocab")), P("mp", ("dp", "vocab")), P()),
        out_specs=(P("mp"), P("dp", "mp"), P("mp", ("dp", "vocab"))),
        check_vma=False,
    )
```
